256 devices in a mesh: gx: 4 (over x), gy: 64 (over z, y, core).
Axes of the slice: x: 4, y: 4, z: 8, core: 2. Of those that a mesh axis runs over, the one named last changes fastest.
Arguments:
- right_side: float32 [4096, 64, 128], P(('gx', 'gy')), may hold values from -6 to 6
- diagonal_matrices: float32 [4096, 64, 64], P(('gx', 'gy')), as said below
- nearby_coupling_blocks: float32 [4096, 4, 64, 64], P(('gx', 'gy'))
- neighbors: int32 [4096, 4], P(('gx', 'gy')), may hold values from 0 to 4095, as said below
- pairs: int32 [256, 3, 2, 8], P(('gx', 'gy')), may hold values from -1 to 15, as said below
- remote_coupling_blocks: float32 [256, 3, 8, 64, 64], P(('gx', 'gy'))
Outputs:
- solution: float32 [4096, 64, 128], P(('gx', 'gy'))
- residual: float32 [4096, 64, 128], P(('gx', 'gy'))
The draws below stay inside these ranges and needn't reach their ends.
Inputs may be any that keep to these rules, and one draw needn't show every extreme that they name: Every neighbour of a block lies in the block's own range of 16 blocks, is not the block itself, and the pattern is symmetric slot by slot: if neighbors[i, k] = j then neighbors[j, k] = i. For device d and level e, with partner p = d xor 2^e: pairs[d, e, 0] lists distinct local blocks of d and pairs[d, e, 1] local blocks of p, with pairs[p, e, 0, t] = pairs[d, e, 1, t] and pairs[p, e, 1, t] = pairs[d, e, 0, t]; a pair of devices uses the same leading count c of slots, the rest are -1 in both rows; at every level some pair uses all 8 slots. The operator assembled from diagonal_matrices, nearby_coupling_blocks and remote_coupling_blocks is symmetric and positive definite.
All inputs are finite; a program needn't handle non-finite values.
Results may differ from the reference program's by a relative error of at most 0.0003.
Values sent between devices are 32-bit elements; how exact they have to be, the bound alone decides.
A program may use at most 64 MiB of HBM per device.

```python
import math
import jax
import jax.numpy as jnp
from jax import lax

WIDTH = 64
BLOCKS_DEV = 16
RHS = 128
LOCAL = 4
CROSS = 3
ITERS = 3
SLOTS = 8
NDEV = 256
NBLOCKS = 4096


def spread_scale():
    return 0.6 * math.sqrt(3.0 / (WIDTH * (LOCAL + 4)))


def local_masks(key):
    return jax.random.randint(jax.random.fold_in(key, 101), (NDEV, LOCAL), 1, BLOCKS_DEV, dtype=jnp.int32)


def neighbor_ids(key):
    xor_masks = local_masks(key)
    row_ids = jnp.arange(NBLOCKS, dtype=jnp.int32)
    owner_dev = row_ids // BLOCKS_DEV
    inner_idx = row_ids % BLOCKS_DEV
    return owner_dev[:, None] * BLOCKS_DEV + jnp.bitwise_xor(inner_idx[:, None], xor_masks[owner_dev])


def partner_table():
    devices = jnp.arange(NDEV, dtype=jnp.int32)
    levels = jnp.arange(CROSS, dtype=jnp.int32)
    return jnp.bitwise_xor(devices[:, None], jnp.left_shift(jnp.int32(1), levels)[None, :])


def pair_lists(key):
    key = jax.random.fold_in(key, 202)
    devices = jnp.arange(NDEV, dtype=jnp.int32)
    levels = jnp.arange(CROSS, dtype=jnp.int32)
    partner = partner_table()

    def one_perm(device, octree_bit_depth):
        sub_key = jax.random.fold_in(jax.random.fold_in(key, device), octree_bit_depth)
        return jax.random.permutation(sub_key, BLOCKS_DEV).astype(jnp.int32)
    shuffles = jax.vmap(lambda device: jax.vmap(lambda octree_bit_depth: one_perm(device, octree_bit_depth))(levels))(devices)
    counts = jax.random.randint(jax.random.fold_in(key, 7), (NDEV, CROSS), max(1, SLOTS // 3), SLOTS + 1, dtype=jnp.int32)
    full_dev = jax.random.randint(jax.random.fold_in(key, 8), (CROSS,), 0, NDEV, dtype=jnp.int32)
    full_lower = jnp.minimum(full_dev, jnp.bitwise_xor(full_dev, jnp.left_shift(jnp.int32(1), levels)))
    counts = jnp.where(devices[:, None] == full_lower[None, :], SLOTS, counts)
    lower_dev = jnp.minimum(devices[:, None], partner)
    live_count = counts[lower_dev, levels[None, :]]
    own_slot = shuffles[:, :, :SLOTS]
    far_slot = shuffles[partner, levels[None, :], :SLOTS]
    live_slot = jnp.arange(SLOTS, dtype=jnp.int32)[None, None, :] < live_count[:, :, None]
    own_slot = jnp.where(live_slot, own_slot, -1)
    far_slot = jnp.where(live_slot, far_slot, -1)
    return jnp.stack([own_slot, far_slot], axis=2).astype(jnp.int32)


def draw_neighbors(key, part):
    return neighbor_ids(key)


def draw_pairs(key, part):
    return pair_lists(key)


def draw_nearby_coupling_blocks(key, part):
    neighbor = neighbor_ids(key)
    key = jax.random.fold_in(key, 3)
    spread = spread_scale()
    raw_blocks = jax.random.uniform(key, (NBLOCKS, LOCAL, WIDTH, WIDTH), jnp.float32, -spread, spread)
    mirror = jnp.swapaxes(raw_blocks[neighbor, jnp.arange(LOCAL, dtype=jnp.int32)[None, :]], -1, -2)
    lower_row = jnp.arange(NBLOCKS, dtype=jnp.int32)[:, None] < neighbor
    return jnp.where(lower_row[:, :, None, None], raw_blocks, mirror)


def draw_remote_coupling_blocks(key, part):
    key = jax.random.fold_in(key, 4)
    spread = spread_scale()
    raw_blocks = jax.random.uniform(key, (NDEV, CROSS, SLOTS, WIDTH, WIDTH), jnp.float32, -spread, spread)
    devices = jnp.arange(NDEV, dtype=jnp.int32)
    levels = jnp.arange(CROSS, dtype=jnp.int32)
    partner = partner_table()
    lower_dev = jnp.minimum(devices[:, None], partner)
    mirror = raw_blocks[lower_dev, levels[None, :]]
    flipped = devices[:, None] > partner
    return jnp.where(flipped[:, :, None, None, None], jnp.swapaxes(mirror, -1, -2), mirror)


def draw_diagonal_matrices(key, part):
    key = jax.random.fold_in(key, 5)
    spread = spread_scale()
    raw_blocks = jax.random.uniform(key, (NBLOCKS, WIDTH, WIDTH), jnp.float32, -spread, spread)
    symmetric = 0.5 * (raw_blocks + jnp.swapaxes(raw_blocks, -1, -2))
    level_key = jax.random.fold_in(key, 6)
    diag_level = jnp.exp(jax.random.uniform(level_key, (NBLOCKS, WIDTH), jnp.float32, math.log(1.8), math.log(8.0)))
    identity = jnp.eye(WIDTH, dtype=jnp.float32)
    return symmetric + identity[None, :, :] * diag_level[:, :, None]


def steps_of(key, extent, cuts, least, largest):
    def one(axis_at, parts):
        heights = jax.random.uniform(jax.random.fold_in(jax.random.fold_in(key, 6), axis_at), (parts,), jnp.float32, least / len(cuts), largest / len(cuts))
        return jnp.repeat(jnp.exp(heights), extent[axis_at] // parts).reshape((-1,) + (1,) * (len(extent) - axis_at - 1))

    level = one(*cuts[0])
    for cut in cuts[1:]:
        level = level * one(*cut)
    return level


def bell_draw(key, dims, scale, most, pieces=(), kind=jnp.bfloat16):
    array = jax.random.normal(key, dims, jnp.float32) * scale
    if len(pieces) > 0:
        array = steps_of(key, dims, pieces, -0.22, 0.18) * array
    return jnp.clip(array, min=-most, max=most).astype(kind)


def setup_inputs(seed: int = 0) -> dict:
    key_of = jax.random.split(jax.random.key(seed), 7)
    right_side = bell_draw(key_of[0], (NBLOCKS, WIDTH, RHS), 1.0, 6.0, ((0, 256),), jnp.float32)
    diagonal_matrices = draw_diagonal_matrices(jax.random.fold_in(key_of[6], 71), 0)
    nearby_coupling_blocks = draw_nearby_coupling_blocks(jax.random.fold_in(key_of[6], 71), 0)
    neighbors = draw_neighbors(jax.random.fold_in(key_of[6], 71), 0)
    pairs = draw_pairs(jax.random.fold_in(key_of[6], 71), 0)
    remote_coupling_blocks = draw_remote_coupling_blocks(jax.random.fold_in(key_of[6], 71), 0)
    return dict(right_side=right_side, diagonal_matrices=diagonal_matrices, nearby_coupling_blocks=nearby_coupling_blocks, neighbors=neighbors, pairs=pairs, remote_coupling_blocks=remote_coupling_blocks)


EXACT_ACCURACY = lax.Precision.HIGHEST


def apply_operator(input_vector, diagonal_matrices, nearby_coupling_blocks, neighbors, pairs, remote_coupling_blocks):
    operator_result = jnp.einsum('ejg,egw->ejw', diagonal_matrices, input_vector, precision=EXACT_ACCURACY)
    for position_index in range(LOCAL):
        fetched_values = input_vector[neighbors[:, position_index]]
        operator_result = operator_result + jnp.einsum('ejg,egw->ejw', nearby_coupling_blocks[:, position_index], fetched_values, precision=EXACT_ACCURACY)
    devices = jnp.arange(NDEV, dtype=jnp.int32)
    for octree_bit_depth in range(CROSS):
        partner = jnp.bitwise_xor(devices, jnp.int32(2 ** octree_bit_depth))
        own_slot = pairs[:, octree_bit_depth, 0]
        far_slot = pairs[:, octree_bit_depth, 1]
        live_slot = (own_slot >= 0).astype(jnp.float32)
        row_ids = devices[:, None] * BLOCKS_DEV + jnp.maximum(own_slot, 0)
        col_ids = partner[:, None] * BLOCKS_DEV + jnp.maximum(far_slot, 0)
        fetched_values = input_vector[col_ids] * live_slot[:, :, None, None]
        coupled_output = jnp.einsum('dsab,dsbr->dsar', remote_coupling_blocks[:, octree_bit_depth], fetched_values, precision=EXACT_ACCURACY)
        operator_result = operator_result.at[row_ids.reshape(-1)].add(coupled_output.reshape(-1, WIDTH, RHS))
    return operator_result


def reference(right_side, diagonal_matrices, nearby_coupling_blocks, neighbors, pairs, remote_coupling_blocks):
    def operate(input_vector):
        return apply_operator(input_vector, diagonal_matrices, nearby_coupling_blocks, neighbors, pairs, remote_coupling_blocks)

    solution = jnp.zeros_like(right_side)
    residual = right_side
    res_image = operate(residual)
    direction = residual
    dir_image = res_image
    dir_image2 = res_image
    gamma_prev = None
    step_prev = None
    for iteration in range(ITERS):
        gamma_now = jnp.sum(residual * residual, axis=(0, 1))
        delta_now = jnp.sum(res_image * residual, axis=(0, 1))
        res_image2 = operate(res_image)
        if iteration == 0:
            step_len = gamma_now / delta_now
            direction = residual
            dir_image = res_image
            dir_image2 = res_image2
        else:
            ratio_now = gamma_now / gamma_prev
            step_len = gamma_now / (delta_now - ratio_now * gamma_now / step_prev)
            direction = residual + ratio_now[None, None, :] * direction
            dir_image = res_image + ratio_now[None, None, :] * dir_image
            dir_image2 = res_image2 + ratio_now[None, None, :] * dir_image2
        solution = solution + step_len[None, None, :] * direction
        residual = residual - step_len[None, None, :] * dir_image
        res_image = res_image - step_len[None, None, :] * dir_image2
        gamma_prev = gamma_now
        step_prev = step_len
    return solution, residual
```

```python
import functools

import jax
import jax.numpy as jnp
from jax import lax
from jax.experimental import pallas as pl
from jax.experimental.pallas import tpu as pltpu
from jax.sharding import PartitionSpec as P

CROSS = 3
SLOTS = 8
HALF = SLOTS // 2
LOCAL = 4
BLOCKS = 16
WIDTH = 64
RHS = 128
SOURCES = LOCAL + 1
DEPTH = 3 * WIDTH
MESH = pl.DeviceIdType.MESH
LEVEL_ORDER = (2, 1, 0)


def tree_sum(parts):
    while len(parts) > 1:
        parts = [parts[i] + parts[i + 1] for i in range(0, len(parts), 2)]
    return parts[0]


def split(value):
    high = value.astype(jnp.bfloat16)
    low = (value - high.astype(jnp.float32)).astype(jnp.bfloat16)
    return high, low


def fold(value):
    return jnp.sum(value.reshape(WIDTH // 8, 8, RHS), axis=0)


def kernel(
    nx, nz,
    neighbors, pairs, right_side, diagonal, nearby, remote,
    solution, residual,
    w0, w1, z0, z1, r1, x_high, x_low, near_lhs, far_lhs, coupled,
    sent, received, first_sums, second_sums, inverse,
    send_sem, recv_sem, first_send, first_recv, second_send, second_recv,
):
    gx = lax.axis_index("gx")
    gy = lax.axis_index("gy")
    z, y, core = gy // 8, (gy // 2) % 4, gy % 2
    n1, n2 = 2 * nz, 4 * nx
    me1, me2 = z * 2 + core, gx * 4 + y

    def first_peer(k):
        other = jnp.bitwise_xor(me1, k)
        return gx, ((other // 2) * 4 + y) * 2 + other % 2

    def second_peer(k):
        other = jnp.bitwise_xor(me2, k)
        return other // 4, (z * 4 + other % 4) * 2 + core

    barrier = pltpu.get_barrier_semaphore()

    def greet(peer):
        def one(k, carry):
            pl.semaphore_signal(barrier, inc=1, device_id=peer(k), device_id_type=MESH)
            return carry
        return one

    lax.fori_loop(1, n1, greet(first_peer), 0)
    lax.fori_loop(1, n2, greet(second_peer), 0)
    pl.semaphore_wait(barrier, n1 + n2 - 2)

    bits = [(gy // (1 << e)) % 2 for e in range(CROSS)]

    def slot_copy(op, e, t):
        return pltpu.make_async_remote_copy(
            src_ref=sent.at[op, e, t],
            dst_ref=received.at[op, e, t],
            send_sem=send_sem.at[op, e, t],
            recv_sem=recv_sem.at[op, e, t],
            device_id=(gx, jnp.bitwise_xor(gy, 1 << e)),
            device_id_type=MESH,
        )

    def send_all(op, source):
        for half in range(2):
            def one(q, carry):
                for e in LEVEL_ORDER:
                    base = HALF * (1 - bits[e]) if half == 0 else HALF * bits[e]
                    t = base + q
                    own = jnp.maximum(pairs[0, e, 0, t], 0)
                    sent[op, e, t] = source[own]
                    slot_copy(op, e, t).start()
                return carry
            lax.fori_loop(0, HALF, one, 0)

    def sum_copy(index, stage, k):
        buffer, sends, recvs, peer = (
            (first_sums, first_send, first_recv, first_peer),
            (second_sums, second_send, second_recv, second_peer),
        )[stage]
        return pltpu.make_async_remote_copy(
            src_ref=buffer.at[index, 0],
            dst_ref=buffer.at[index, k],
            send_sem=sends.at[index],
            recv_sem=recvs.at[index],
            device_id=peer(k),
            device_id_type=MESH,
        )

    def sum_all_wait(index, stage):
        buffer, sends, recvs, peer = (
            (first_sums, first_send, first_recv, first_peer),
            (second_sums, second_send, second_recv, second_peer),
        )[stage]
        n = (n1, n2)[stage]
        return pltpu.make_async_remote_copy(
            src_ref=buffer.at[index, pl.ds(1, n - 1)],
            dst_ref=buffer.at[index, pl.ds(1, n - 1)],
            send_sem=sends.at[index],
            recv_sem=recvs.at[index],
            device_id=peer(1),
            device_id_type=MESH,
        )

    def sum_start(index, stage, value):
        buffer, n = ((first_sums, n1), (second_sums, n2))[stage]
        buffer[index, 0] = value

        def one(k, carry):
            sum_copy(index, stage, k).start()
            return carry
        lax.fori_loop(1, n, one, 0)

    def sum_finish(index, stage):
        buffer, n = ((first_sums, n1), (second_sums, n2))[stage]
        sum_all_wait(index, stage).wait_recv()
        return tree_sum([buffer[index, k] for k in range(n)])

    def rows_of(values):
        rows = [jnp.sum(v, axis=0, keepdims=True) for v in values]
        rows += [jnp.zeros((8 - len(rows), RHS), jnp.float32)] if len(rows) < 8 else []
        return jnp.concatenate(rows, axis=0)

    def split_all(source):
        def one(i, carry):
            high, low = split(source[i])
            x_high[i] = high
            x_low[i] = low
            return carry
        lax.fori_loop(0, BLOCKS, one, 0)

    def near_product(i):
        sources = [i] + [jnp.bitwise_and(neighbors[i, k], BLOCKS - 1) for k in range(LOCAL)]
        highs = [x_high[j] for j in sources]
        lows = [x_low[j] for j in sources]
        rhs = jnp.concatenate([h for high in highs for h in (high, high)] + lows, axis=0)
        return jnp.dot(near_lhs[i][:, : SOURCES * DEPTH], rhs, preferred_element_type=jnp.float32)

    def far_product(op, e, t):
        slot_copy(op, e, t).wait_recv()
        high, low = split(received[op, e, t])
        rhs = jnp.concatenate([high, high, low], axis=0)
        product = jnp.dot(far_lhs[e, t][:, :DEPTH], rhs, preferred_element_type=jnp.float32)
        coupled[e, t] = product
        return product

    def far_half(op, half):
        def one(q, carry):
            for e in reversed(LEVEL_ORDER):
                far_product(op, e, q + (HALF * bits[e] if half == 0 else HALF * (1 - bits[e])))
            return carry
        lax.fori_loop(0, HALF, one, 0)

    def far_rows(i):
        return [coupled[e, inverse[e * BLOCKS + i]] for e in range(CROSS)]

    zero = jnp.zeros((8, RHS), jnp.float32)

    send_all(0, right_side)

    lane = lax.broadcasted_iota(jnp.int32, (WIDTH, 2 * WIDTH), 1)

    def both(block):
        twice = jnp.concatenate([block, block], axis=1)
        high = twice.astype(jnp.bfloat16).astype(jnp.float32)
        return jnp.where(lane < WIDTH, high, twice - high).astype(jnp.bfloat16)

    def near_setup(i, carry):
        blocks = [diagonal[i]] + [nearby[i, k] for k in range(LOCAL)]
        for s, block in enumerate(blocks):
            near_lhs[i, :, pl.ds(s * 2 * WIDTH, 2 * WIDTH)] = both(block)
        for s in range(0, SOURCES, 2):
            pair = jnp.concatenate([blocks[s], blocks[min(s + 1, SOURCES - 1)]], axis=1)
            near_lhs[i, :, pl.ds((SOURCES * 2 + s) * WIDTH, 2 * WIDTH)] = pair.astype(jnp.bfloat16)
        return carry

    lax.fori_loop(0, BLOCKS, near_setup, 0)

    def far_setup(t, carry):
        for e in range(CROSS):
            block = remote[0, e, t]
            far_lhs[e, t, :, pl.ds(0, 2 * WIDTH)] = both(block)
            twice = jnp.concatenate([block, block], axis=1)
            far_lhs[e, t, :, pl.ds(2 * WIDTH, 2 * WIDTH)] = twice.astype(jnp.bfloat16)
        return carry

    lax.fori_loop(0, SLOTS, far_setup, 0)

    for e in range(CROSS):
        coupled[e, SLOTS] = jnp.zeros((WIDTH, RHS), jnp.float32)
        owns = [pairs[0, e, 0, t] for t in range(SLOTS)]

        def invert(i, carry):
            found = jnp.int32(SLOTS)
            for t in range(SLOTS):
                found = jnp.where(owns[t] == i, jnp.int32(t), found)
            inverse[e * BLOCKS + i] = found
            return carry
        lax.fori_loop(0, BLOCKS, invert, 0)

    split_all(right_side)

    def w0_near(i, carry):
        w0[i] = near_product(i)
        return carry

    lax.fori_loop(0, BLOCKS, w0_near, 0)
    far_half(0, 0)
    far_half(0, 1)

    def w0_join(i, carry):
        gamma, delta = carry
        r = right_side[i]
        w = w0[i] + tree_sum(far_rows(i) + [jnp.zeros_like(r)])
        w0[i] = w
        return gamma + fold(r * r), delta + fold(w * r)

    gamma, delta = lax.fori_loop(0, BLOCKS, w0_join, (zero, zero))

    send_all(1, w0)
    sum_start(0, 0, rows_of([gamma, delta]))
    split_all(w0)

    def z0_near(i, carry):
        z0[i] = near_product(i)
        return carry

    lax.fori_loop(0, BLOCKS, z0_near, 0)
    sum_start(0, 1, sum_finish(0, 0))
    far_half(1, 0)
    far_half(1, 1)
    totals = sum_finish(0, 1)
    gamma0, delta0 = totals[0:1], totals[1:2]
    step0 = gamma0 / delta0

    def z0_join(i, carry):
        zz = z0[i] + tree_sum(far_rows(i) + [jnp.zeros((WIDTH, RHS), jnp.float32)])
        z0[i] = zz
        w1[i] = w0[i] - step0 * zz
        return carry

    lax.fori_loop(0, BLOCKS, z0_join, 0)

    send_all(2, w1)

    def gram(i, carry):
        wa, wb, zz = w0[i], w1[i], z0[i]
        r = right_side[i] - step0 * wa
        r1[i] = r
        terms = (r * r, r * wb, r * wa, wb * wb, wb * wa, wa * wa, wb * zz, wa * zz)
        return tuple(c + fold(t) for c, t in zip(carry, terms))

    sums = lax.fori_loop(0, BLOCKS, gram, (zero,) * 8)
    sum_start(1, 0, rows_of(sums))
    split_all(w1)

    def z1_near(i, energy):
        product = near_product(i)
        z1[i] = product
        return energy + fold(product * w1[i])

    energy = lax.fori_loop(0, BLOCKS, z1_near, zero)

    def energy_half(q, carry):
        for e in reversed(LEVEL_ORDER):
            t = q + HALF * bits[e]
            product = far_product(2, e, t)
            twice = jnp.where(pairs[0, e, 0, t] >= 0, 2.0 * fold(product * sent[2, e, t]), 0.0)
            carry = carry + twice
        return carry

    energy = lax.fori_loop(0, HALF, energy_half, energy)
    sum_start(2, 0, rows_of([energy]))
    sum_start(1, 1, sum_finish(1, 0))
    far_half(2, 1)
    sum_start(2, 1, sum_finish(2, 0))
    totals = sum_finish(1, 1)
    gamma1, delta1, rw0, w1w1, w1w0, w0w0, w1z0, w0z0 = [totals[k : k + 1] for k in range(8)]
    ratio1 = gamma1 / gamma0
    step1 = gamma1 / (delta1 - ratio1 * gamma1 / step0)

    def z1_join(i, carry):
        zz = z1[i] + tree_sum(far_rows(i) + [jnp.zeros((WIDTH, RHS), jnp.float32)])
        r, wa, wb, r0 = r1[i], w0[i], w1[i], right_side[i]
        p1 = r + ratio1 * r0
        ap1 = wb + ratio1 * wa
        solution[i] = step0 * r0 + step1 * p1
        residual[i] = r - step1 * ap1
        z1[i] = wb - step1 * (zz + ratio1 * z0[i])
        r1[i] = p1
        w1[i] = ap1
        return carry

    lax.fori_loop(0, BLOCKS, z1_join, 0)

    w1aw1 = sum_finish(2, 1)[0:1]
    gamma2 = (
        gamma1
        - 2.0 * step1 * (delta1 + ratio1 * rw0)
        + step1 * step1 * (w1w1 + 2.0 * ratio1 * w1w0 + ratio1 * ratio1 * w0w0)
    )
    delta2 = (
        delta1
        - 2.0 * step1 * (w1w1 + ratio1 * w1w0)
        + step1 * step1 * (w1aw1 + 2.0 * ratio1 * w1z0 + ratio1 * ratio1 * w0z0)
    )
    ratio2 = gamma2 / gamma1
    step2 = gamma2 / (delta2 - ratio2 * gamma2 / step1)

    def last(i, carry):
        r2 = residual[i]
        solution[i] = solution[i] + step2 * (r2 + ratio2 * r1[i])
        residual[i] = r2 - step2 * (z1[i] + ratio2 * w1[i])
        return carry

    lax.fori_loop(0, BLOCKS, last, 0)

    for op in range(3):
        def drain(t, carry):
            for e in range(CROSS):
                slot_copy(op, e, t).wait_send()
            return carry
        lax.fori_loop(0, SLOTS, drain, 0)
        for stage in range(2):
            sum_all_wait(op, stage).wait_send()


def solution(mesh):
    nx, nz = mesh.shape["gx"], mesh.shape["gy"] // 8
    n1, n2 = 2 * nz, 4 * nx

    def local(right_side, diagonal_matrices, nearby_coupling_blocks, neighbors, pairs, remote_coupling_blocks):
        field = (BLOCKS, WIDTH, RHS)
        vmem = pl.BlockSpec(memory_space=pltpu.VMEM)
        smem = pl.BlockSpec(memory_space=pltpu.SMEM)
        f32, bf16 = jnp.float32, jnp.bfloat16
        return pl.pallas_call(
            functools.partial(kernel, nx, nz),
            out_shape=(jax.ShapeDtypeStruct(field, f32), jax.ShapeDtypeStruct(field, f32)),
            in_specs=[smem, smem, vmem, vmem, vmem, vmem],
            out_specs=(vmem, vmem),
            scratch_shapes=[pltpu.VMEM(field, f32)] * 5
            + [
                pltpu.VMEM(field, bf16),
                pltpu.VMEM(field, bf16),
                pltpu.VMEM((BLOCKS, WIDTH, 1024), bf16),
                pltpu.VMEM((CROSS, SLOTS, WIDTH, 256), bf16),
                pltpu.VMEM((CROSS, SLOTS + 1, WIDTH, RHS), f32),
                pltpu.VMEM((3, CROSS, SLOTS, WIDTH, RHS), f32),
                pltpu.VMEM((3, CROSS, SLOTS, WIDTH, RHS), f32),
                pltpu.VMEM((3, n1, 8, RHS), f32),
                pltpu.VMEM((3, n2, 8, RHS), f32),
                pltpu.SMEM((CROSS * BLOCKS,), jnp.int32),
                pltpu.SemaphoreType.DMA((3, CROSS, SLOTS)),
                pltpu.SemaphoreType.DMA((3, CROSS, SLOTS)),
                pltpu.SemaphoreType.DMA((3,)),
                pltpu.SemaphoreType.DMA((3,)),
                pltpu.SemaphoreType.DMA((3,)),
                pltpu.SemaphoreType.DMA((3,)),
            ],
            compiler_params=pltpu.CompilerParams(
                collective_id=0, has_side_effects=True, vmem_limit_bytes=40 * 1024 * 1024
            ),
            name="relay",
        )(neighbors, pairs, right_side, diagonal_matrices, nearby_coupling_blocks, remote_coupling_blocks)

    wide = P(("gx", "gy"), None, None)
    return jax.shard_map(
        local,
        mesh=mesh,
        in_specs=(
            wide,
            wide,
            P(("gx", "gy"), None, None, None),
            P(("gx", "gy"), None),
            P(("gx", "gy"), None, None, None),
            P(("gx", "gy"), None, None, None, None),
        ),
        out_specs=(wide, wide),
        check_vma=False,
    )
```

```python
import functools

import jax
import jax.numpy as jnp
from jax import lax
from jax.experimental import pallas as pl
from jax.experimental.pallas import tpu as pltpu
from jax.sharding import PartitionSpec as P

CROSS = 3
SLOTS = 8
HALF = SLOTS // 2
LOCAL = 4
BLOCKS = 16
WIDTH = 64
RHS = 128
SOURCES = LOCAL + 1
DEPTH = 3 * WIDTH
MESH = pl.DeviceIdType.MESH
LEVEL_ORDER = (2, 1, 0)


def tree_sum(parts):
    while len(parts) > 1:
        parts = [parts[i] + parts[i + 1] for i in range(0, len(parts), 2)]
    return parts[0]


def split(value):
    high = value.astype(jnp.bfloat16)
    low = (value - high.astype(jnp.float32)).astype(jnp.bfloat16)
    return high, low


def fold(value):
    return jnp.sum(value.reshape(WIDTH // 8, 8, RHS), axis=0)


def kernel(
    nx, nz,
    neighbors_in, pairs_in, right_side_in, diagonal_in, nearby_in, remote_in,
    solution, residual,
    neighbors, pairs, right_side, diagonal, nearby, remote,
    w0, w1, z0, z1, r1, x_high, x_low, near_lhs, far_lhs, coupled,
    sent, received, first_sums, second_sums, inverse,
    in_sem, send_sem, recv_sem, first_send, first_recv, second_send, second_recv,
):
    gx = lax.axis_index("gx")
    gy = lax.axis_index("gy")
    z, y, core = gy // 8, (gy // 2) % 4, gy % 2
    n1, n2 = 2 * nz, 4 * nx
    me1, me2 = z * 2 + core, gx * 4 + y

    def first_peer(k):
        other = jnp.bitwise_xor(me1, k)
        return gx, ((other // 2) * 4 + y) * 2 + other % 2

    def second_peer(k):
        other = jnp.bitwise_xor(me2, k)
        return other // 4, (z * 4 + other % 4) * 2 + core

    barrier = pltpu.get_barrier_semaphore()

    def greet(peer):
        def one(k, carry):
            pl.semaphore_signal(barrier, inc=1, device_id=peer(k), device_id_type=MESH)
            return carry
        return one

    inputs = [
        pltpu.make_async_copy(source, target, in_sem.at[n])
        for n, (source, target) in enumerate(
            (
                (pairs_in, pairs),
                (right_side_in, right_side),
                (neighbors_in, neighbors),
                (diagonal_in, diagonal),
                (nearby_in, nearby),
                (remote_in, remote),
            )
        )
    ]
    for copy in inputs:
        copy.start()
    lax.fori_loop(1, n1, greet(first_peer), 0)
    lax.fori_loop(1, n2, greet(second_peer), 0)

    bits = [(gy // (1 << e)) % 2 for e in range(CROSS)]

    def slot_copy(op, e, t):
        return pltpu.make_async_remote_copy(
            src_ref=sent.at[op, e, t],
            dst_ref=received.at[op, e, t],
            send_sem=send_sem.at[op, e, t],
            recv_sem=recv_sem.at[op, e, t],
            device_id=(gx, jnp.bitwise_xor(gy, 1 << e)),
            device_id_type=MESH,
        )

    def slot_of(half, q, e):
        return q + (HALF * (1 - bits[e]) if half == 0 else HALF * bits[e])

    def gather(op, half, q, block):
        for e in LEVEL_ORDER:
            t = slot_of(half, q, e)
            sent[op, e, t] = block(jnp.maximum(pairs[0, e, 0, t], 0))

    def send(op, half, q):
        for e in LEVEL_ORDER:
            slot_copy(op, e, slot_of(half, q, e)).start()

    def send_all(op, block):
        for half in range(2):
            def one(q, carry):
                gather(op, half, q, block)
                send(op, half, q)
                return carry
            lax.fori_loop(0, HALF, one, 0, unroll=2)

    def sum_copy(index, stage, k):
        buffer, sends, recvs, peer = (
            (first_sums, first_send, first_recv, first_peer),
            (second_sums, second_send, second_recv, second_peer),
        )[stage]
        return pltpu.make_async_remote_copy(
            src_ref=buffer.at[index, 0],
            dst_ref=buffer.at[index, k],
            send_sem=sends.at[index],
            recv_sem=recvs.at[index],
            device_id=peer(k),
            device_id_type=MESH,
        )

    def sum_all_wait(index, stage):
        buffer, sends, recvs, peer = (
            (first_sums, first_send, first_recv, first_peer),
            (second_sums, second_send, second_recv, second_peer),
        )[stage]
        n = (n1, n2)[stage]
        return pltpu.make_async_remote_copy(
            src_ref=buffer.at[index, pl.ds(1, n - 1)],
            dst_ref=buffer.at[index, pl.ds(1, n - 1)],
            send_sem=sends.at[index],
            recv_sem=recvs.at[index],
            device_id=peer(1),
            device_id_type=MESH,
        )

    def sum_start(index, stage, value):
        buffer, n = ((first_sums, n1), (second_sums, n2))[stage]
        buffer[index, 0] = value

        def one(k, carry):
            sum_copy(index, stage, k).start()
            return carry
        lax.fori_loop(1, n, one, 0)

    def sum_finish(index, stage):
        buffer, n = ((first_sums, n1), (second_sums, n2))[stage]
        sum_all_wait(index, stage).wait_recv()
        return tree_sum([buffer[index, k] for k in range(n)])

    def rows_of(values):
        rows = [jnp.sum(v, axis=0, keepdims=True) for v in values]
        rows += [jnp.zeros((8 - len(rows), RHS), jnp.float32)] if len(rows) < 8 else []
        return jnp.concatenate(rows, axis=0)

    def put(i, value):
        high, low = split(value)
        x_high[i] = high
        x_low[i] = low

    def near_product(i):
        sources = [i] + [jnp.bitwise_and(neighbors[k, i], BLOCKS - 1) for k in range(LOCAL)]
        highs = [x_high[j] for j in sources]
        lows = [x_low[j] for j in sources]
        rhs = jnp.concatenate([h for high in highs for h in (high, high)] + lows, axis=0)
        return jnp.dot(near_lhs[i][:, : SOURCES * DEPTH], rhs, preferred_element_type=jnp.float32)

    def far_product(op, e, t):
        high, low = split(received[op, e, t])
        rhs = jnp.concatenate([high, high, low], axis=0)
        product = jnp.dot(far_lhs[e, t][:, :DEPTH], rhs, preferred_element_type=jnp.float32)
        coupled[e, t] = product
        return product

    def far_step(op, half, q):
        slots = [slot_of(1 - half, q, e) for e in range(CROSS)]
        for e in range(CROSS):
            slot_copy(op, e, slots[e]).wait_recv()
        return slots, [far_product(op, e, slots[e]) for e in range(CROSS)]

    def far_half(op, half):
        def one(q, carry):
            far_step(op, half, q)
            return carry
        lax.fori_loop(0, HALF, one, 0, unroll=2)

    def join(near, i):
        a, b, c = [coupled[e, inverse[e * BLOCKS + i]] for e in range(CROSS)]
        return (near[i] + a) + (b + c)

    zero = jnp.zeros((8, RHS), jnp.float32)

    inputs[0].wait()
    inputs[1].wait()
    for half in range(2):
        def prepare(q, carry):
            gather(0, half, q, lambda j: right_side[j])
            return carry
        lax.fori_loop(0, HALF, prepare, 0)
    pl.semaphore_wait(barrier, n1 + n2 - 2)
    for half in range(2):
        def begin(q, carry):
            send(0, half, q)
            return carry
        lax.fori_loop(0, HALF, begin, 0)
    for copy in inputs[2:]:
        copy.wait()

    lane = lax.broadcasted_iota(jnp.int32, (WIDTH, 2 * WIDTH), 1)

    def both(block):
        twice = jnp.concatenate([block, block], axis=1)
        high = twice.astype(jnp.bfloat16).astype(jnp.float32)
        return jnp.where(lane < WIDTH, high, twice - high).astype(jnp.bfloat16)

    def near_setup(i, carry):
        blocks = [diagonal[i]] + [nearby[i, k] for k in range(LOCAL)]
        for s, block in enumerate(blocks):
            near_lhs[i, :, pl.ds(s * 2 * WIDTH, 2 * WIDTH)] = both(block)
        for s in range(0, SOURCES, 2):
            pair = jnp.concatenate([blocks[s], blocks[min(s + 1, SOURCES - 1)]], axis=1)
            near_lhs[i, :, pl.ds((SOURCES * 2 + s) * WIDTH, 2 * WIDTH)] = pair.astype(jnp.bfloat16)
        return carry

    lax.fori_loop(0, BLOCKS, near_setup, 0, unroll=2)

    def far_setup(t, carry):
        for e in range(CROSS):
            block = remote[0, e, t]
            far_lhs[e, t, :, pl.ds(0, 2 * WIDTH)] = both(block)
            twice = jnp.concatenate([block, block], axis=1)
            far_lhs[e, t, :, pl.ds(2 * WIDTH, 2 * WIDTH)] = twice.astype(jnp.bfloat16)
        return carry

    lax.fori_loop(0, SLOTS, far_setup, 0, unroll=2)

    for e in range(CROSS):
        coupled[e, SLOTS] = jnp.zeros((WIDTH, RHS), jnp.float32)
        owns = [pairs[0, e, 0, t] for t in range(SLOTS)]

        def invert(i, carry):
            found = jnp.int32(SLOTS)
            for t in range(SLOTS):
                found = jnp.where(owns[t] == i, jnp.int32(t), found)
            inverse[e * BLOCKS + i] = found
            return carry
        lax.fori_loop(0, BLOCKS, invert, 0, unroll=4)

    def first_put(i, carry):
        put(i, right_side[i])
        return carry

    lax.fori_loop(0, BLOCKS, first_put, 0, unroll=4)

    def near_all(target):
        def one(i, carry):
            target[i] = near_product(i)
            return carry
        lax.fori_loop(0, BLOCKS, one, 0, unroll=4)

    near_all(w0)
    far_half(0, 0)
    far_half(0, 1)

    send_all(1, lambda j: join(w0, j))

    def w0_join(i, carry):
        gamma, delta = carry
        r = right_side[i]
        w = join(w0, i)
        w0[i] = w
        put(i, w)
        return gamma + fold(r * r), delta + fold(w * r)

    sums = lax.fori_loop(0, BLOCKS, w0_join, (zero, zero), unroll=4)
    sum_start(0, 0, rows_of(sums))
    near_all(z0)
    sum_start(0, 1, sum_finish(0, 0))
    far_half(1, 0)
    totals = sum_finish(0, 1)
    gamma0, delta0 = totals[0:1], totals[1:2]
    step0 = gamma0 / delta0
    far_half(1, 1)

    send_all(2, lambda j: w0[j] - step0 * join(z0, j))

    def z0_join(i, carry):
        zz, wa = join(z0, i), w0[i]
        wb = wa - step0 * zz
        r = right_side[i] - step0 * wa
        z0[i] = zz
        w1[i] = wb
        r1[i] = r
        put(i, wb)
        terms = (r * r, r * wb, r * wa, wb * wb, wb * wa, wa * wa, wb * zz, wa * zz)
        return tuple(c + fold(t) for c, t in zip(carry, terms))

    sums = lax.fori_loop(0, BLOCKS, z0_join, (zero,) * 8, unroll=2)
    sum_start(1, 0, rows_of(sums))

    def z1_near(i, energy):
        product = near_product(i)
        z1[i] = product
        return energy + fold(product * w1[i])

    energy = lax.fori_loop(0, BLOCKS, z1_near, zero, unroll=4)
    sum_start(1, 1, sum_finish(1, 0))

    def energy_step(q, carry):
        slots, products = far_step(2, 0, q)
        for e in range(CROSS):
            twice = 2.0 * fold(products[e] * sent[2, e, slots[e]])
            carry = carry + jnp.where(pairs[0, e, 0, slots[e]] >= 0, twice, 0.0)
        return carry

    energy = lax.fori_loop(0, HALF, energy_step, energy, unroll=2)
    sum_start(2, 0, rows_of([energy]))
    for q in range(HALF - 1):
        far_step(2, 1, q)
    sum_start(2, 1, sum_finish(2, 0))
    far_step(2, 1, HALF - 1)
    totals = sum_finish(1, 1)
    gamma1, delta1, rw0, w1w1, w1w0, w0w0, w1z0, w0z0 = [totals[k : k + 1] for k in range(8)]
    ratio1 = gamma1 / gamma0
    step1 = gamma1 / (delta1 - ratio1 * gamma1 / step0)

    def z1_join(i, carry):
        zz = join(z1, i)
        r, wa, wb, r0 = r1[i], w0[i], w1[i], right_side[i]
        p1 = r + ratio1 * r0
        ap1 = wb + ratio1 * wa
        solution[i] = step0 * r0 + step1 * p1
        residual[i] = r - step1 * ap1
        z1[i] = wb - step1 * (zz + ratio1 * z0[i])
        r1[i] = p1
        w1[i] = ap1
        return carry

    lax.fori_loop(0, BLOCKS, z1_join, 0, unroll=4)

    w1aw1 = sum_finish(2, 1)[0:1]
    gamma2 = (
        gamma1
        - 2.0 * step1 * (delta1 + ratio1 * rw0)
        + step1 * step1 * (w1w1 + 2.0 * ratio1 * w1w0 + ratio1 * ratio1 * w0w0)
    )
    delta2 = (
        delta1
        - 2.0 * step1 * (w1w1 + ratio1 * w1w0)
        + step1 * step1 * (w1aw1 + 2.0 * ratio1 * w1z0 + ratio1 * ratio1 * w0z0)
    )
    ratio2 = gamma2 / gamma1
    step2 = gamma2 / (delta2 - ratio2 * gamma2 / step1)

    def last(i, carry):
        r2 = residual[i]
        solution[i] = solution[i] + step2 * (r2 + ratio2 * r1[i])
        residual[i] = r2 - step2 * (z1[i] + ratio2 * w1[i])
        return carry

    lax.fori_loop(0, BLOCKS, last, 0, unroll=4)

    for op in range(3):
        def drain(t, carry):
            for e in range(CROSS):
                slot_copy(op, e, t).wait_send()
            return carry
        lax.fori_loop(0, SLOTS, drain, 0)
        for stage in range(2):
            sum_all_wait(op, stage).wait_send()


def solution(mesh):
    nx, nz = mesh.shape["gx"], mesh.shape["gy"] // 8
    n1, n2 = 2 * nz, 4 * nx

    def local(right_side, diagonal_matrices, nearby_coupling_blocks, neighbors, pairs, remote_coupling_blocks):
        field = (BLOCKS, WIDTH, RHS)
        vmem = pl.BlockSpec(memory_space=pltpu.VMEM)
        f32, bf16 = jnp.float32, jnp.bfloat16
        return pl.pallas_call(
            functools.partial(kernel, nx, nz),
            out_shape=(jax.ShapeDtypeStruct(field, f32), jax.ShapeDtypeStruct(field, f32)),
            in_specs=[pl.BlockSpec(memory_space=pl.ANY)] * 6,
            out_specs=(vmem, vmem),
            scratch_shapes=[
                pltpu.SMEM((LOCAL, BLOCKS), jnp.int32),
                pltpu.SMEM(pairs.shape, jnp.int32),
                pltpu.VMEM(field, f32),
                pltpu.VMEM(diagonal_matrices.shape, f32),
                pltpu.VMEM(nearby_coupling_blocks.shape, f32),
                pltpu.VMEM(remote_coupling_blocks.shape, f32),
            ]
            + [pltpu.VMEM(field, f32)] * 5
            + [
                pltpu.VMEM(field, bf16),
                pltpu.VMEM(field, bf16),
                pltpu.VMEM((BLOCKS, WIDTH, 1024), bf16),
                pltpu.VMEM((CROSS, SLOTS, WIDTH, 256), bf16),
                pltpu.VMEM((CROSS, SLOTS + 1, WIDTH, RHS), f32),
                pltpu.VMEM((3, CROSS, SLOTS, WIDTH, RHS), f32),
                pltpu.VMEM((3, CROSS, SLOTS, WIDTH, RHS), f32),
                pltpu.VMEM((3, n1, 8, RHS), f32),
                pltpu.VMEM((3, n2, 8, RHS), f32),
                pltpu.SMEM((CROSS * BLOCKS,), jnp.int32),
                pltpu.SemaphoreType.DMA((6,)),
                pltpu.SemaphoreType.DMA((3, CROSS, SLOTS)),
                pltpu.SemaphoreType.DMA((3, CROSS, SLOTS)),
                pltpu.SemaphoreType.DMA((3,)),
                pltpu.SemaphoreType.DMA((3,)),
                pltpu.SemaphoreType.DMA((3,)),
                pltpu.SemaphoreType.DMA((3,)),
            ],
            compiler_params=pltpu.CompilerParams(
                collective_id=0, has_side_effects=True, vmem_limit_bytes=56 * 1024 * 1024
            ),
            name="relay",
        )(neighbors.T, pairs, right_side, diagonal_matrices, nearby_coupling_blocks, remote_coupling_blocks)

    wide = P(("gx", "gy"), None, None)
    return jax.shard_map(
        local,
        mesh=mesh,
        in_specs=(
            wide,
            wide,
            P(("gx", "gy"), None, None, None),
            P(("gx", "gy"), None),
            P(("gx", "gy"), None, None, None),
            P(("gx", "gy"), None, None, None, None),
        ),
        out_specs=(wide, wide),
        check_vma=False,
    )
```

```python
import functools

import jax
import jax.numpy as jnp
from jax import lax
from jax.experimental import pallas as pl
from jax.experimental.pallas import tpu as pltpu
from jax.sharding import PartitionSpec as P

CROSS = 3
SLOTS = 8
HALF = SLOTS // 2
LOCAL = 4
BLOCKS = 16
WIDTH = 64
RHS = 128
SOURCES = LOCAL + 1
DEPTH = 3 * WIDTH
MESH = pl.DeviceIdType.MESH
LEVEL_ORDER = (2, 1, 0)


def tree_sum(parts):
    while len(parts) > 1:
        parts = [parts[i] + parts[i + 1] for i in range(0, len(parts), 2)]
    return parts[0]


def split(value):
    high = value.astype(jnp.bfloat16)
    low = (value - high.astype(jnp.float32)).astype(jnp.bfloat16)
    return high, low


def fold(value):
    return jnp.sum(value.reshape(WIDTH // 8, 8, RHS), axis=0)


def kernel(
    nx, nz,
    neighbors_in, pairs_in, right_side_in, diagonal_in, nearby_in, remote_in,
    so_far, residual, direction, image, dir_image, last_steps,
    neighbors, pairs, right_side, diagonal, nearby, remote,
    w0, w1, z0, z1, r1, x_high, x_low, near_lhs, far_lhs, coupled,
    sent, received, first_sums, second_sums, inverse,
    in_sem, send_sem, recv_sem, first_send, first_recv, second_send, second_recv,
):
    gx = lax.axis_index("gx")
    gy = lax.axis_index("gy")
    z, y, core = gy >> 3, (gy >> 1) & 3, gy & 1
    n1, n2 = 4 * nx, 2 * nz
    me1, me2 = gx * 4 + y, z * 2 + core

    def first_peer(k):
        other = jnp.bitwise_xor(me1, k)
        return other >> 2, (z << 3) + ((other & 3) << 1) + core

    def second_peer(k):
        other = jnp.bitwise_xor(me2, k)
        return gx, ((other >> 1) << 3) + (y << 1) + (other & 1)

    barrier = pltpu.get_barrier_semaphore()

    def greet(peer):
        def one(k, carry):
            pl.semaphore_signal(barrier, inc=1, device_id=peer(k), device_id_type=MESH)
            return carry
        return one

    inputs = [
        pltpu.make_async_copy(source, target, in_sem.at[n])
        for n, (source, target) in enumerate(
            (
                (pairs_in, pairs),
                (right_side_in, right_side),
                (neighbors_in, neighbors),
                (diagonal_in, diagonal),
                (nearby_in, nearby),
                (remote_in, remote),
            )
        )
    ]
    for copy in inputs:
        copy.start()
    lax.fori_loop(1, n1, greet(first_peer), 0)
    lax.fori_loop(1, n2, greet(second_peer), 0)

    bits = [(gy // (1 << e)) % 2 for e in range(CROSS)]

    def slot_copy(op, e, t):
        return pltpu.make_async_remote_copy(
            src_ref=sent.at[op, e, t],
            dst_ref=received.at[op, e, t],
            send_sem=send_sem.at[op, e, t],
            recv_sem=recv_sem.at[op, e, t],
            device_id=(gx, jnp.bitwise_xor(gy, 1 << e)),
            device_id_type=MESH,
        )

    def slot_of(half, q, e):
        return q + (HALF * (1 - bits[e]) if half == 0 else HALF * bits[e])

    def gather(op, half, q, block):
        for e in LEVEL_ORDER:
            t = slot_of(half, q, e)
            sent[op, e, t] = block(jnp.maximum(pairs[0, e, 0, t], 0))

    def send(op, half, q):
        for e in LEVEL_ORDER:
            slot_copy(op, e, slot_of(half, q, e)).start()

    def send_half(op, half, block):
        def one(q, carry):
            gather(op, half, q, block)
            send(op, half, q)
            return carry
        lax.fori_loop(0, HALF, one, 0, unroll=2)

    def sum_copy(index, stage, k):
        buffer, sends, recvs, peer = (
            (first_sums, first_send, first_recv, first_peer),
            (second_sums, second_send, second_recv, second_peer),
        )[stage]
        return pltpu.make_async_remote_copy(
            src_ref=buffer.at[index, 0],
            dst_ref=buffer.at[index, k],
            send_sem=sends.at[index],
            recv_sem=recvs.at[index],
            device_id=peer(k),
            device_id_type=MESH,
        )

    def sum_all_wait(index, stage):
        buffer, sends, recvs, peer = (
            (first_sums, first_send, first_recv, first_peer),
            (second_sums, second_send, second_recv, second_peer),
        )[stage]
        n = (n1, n2)[stage]
        return pltpu.make_async_remote_copy(
            src_ref=buffer.at[index, pl.ds(1, n - 1)],
            dst_ref=buffer.at[index, pl.ds(1, n - 1)],
            send_sem=sends.at[index],
            recv_sem=recvs.at[index],
            device_id=peer(1),
            device_id_type=MESH,
        )

    def sum_start(index, stage, value):
        buffer, n = ((first_sums, n1), (second_sums, n2))[stage]
        buffer[index, 0] = value

        def one(k, carry):
            sum_copy(index, stage, k).start()
            return carry
        lax.fori_loop(1, n, one, 0)

    def sum_finish(index, stage):
        buffer, n = ((first_sums, n1), (second_sums, n2))[stage]
        sum_all_wait(index, stage).wait_recv()
        return tree_sum([buffer[index, k] for k in range(n)])

    def rows_of(values):
        rows = [jnp.sum(v, axis=0, keepdims=True) for v in values]
        rows += [jnp.zeros((8 - len(rows), RHS), jnp.float32)] if len(rows) < 8 else []
        return jnp.concatenate(rows, axis=0)

    def put(i, value):
        high, low = split(value)
        x_high[i] = high
        x_low[i] = low

    def near_product(i):
        sources = [i] + [jnp.bitwise_and(neighbors[k, i], BLOCKS - 1) for k in range(LOCAL)]
        highs = [x_high[j] for j in sources]
        lows = [x_low[j] for j in sources]
        rhs = jnp.concatenate([h for high in highs for h in (high, high)] + lows, axis=0)
        return jnp.dot(near_lhs[i][:, : SOURCES * DEPTH], rhs, preferred_element_type=jnp.float32)

    def far_product(op, e, t):
        high, low = split(received[op, e, t])
        rhs = jnp.concatenate([high, high, low], axis=0)
        product = jnp.dot(far_lhs[e, t][:, :DEPTH], rhs, preferred_element_type=jnp.float32)
        coupled[e, t] = product
        return product

    def far_step(op, half, q):
        slots = [slot_of(1 - half, q, e) for e in range(CROSS)]
        for e in range(CROSS):
            slot_copy(op, e, slots[e]).wait_recv()
        return slots, [far_product(op, e, slots[e]) for e in range(CROSS)]

    def far_half(op, half):
        def one(q, carry):
            far_step(op, half, q)
            return carry
        lax.fori_loop(0, HALF, one, 0, unroll=2)

    def energy_half(op, source, energy):
        def one(q, carry):
            slots, products = far_step(op, 0, q)
            for e in range(CROSS):
                own = pairs[0, e, 0, slots[e]]
                twice = 2.0 * fold(products[e] * source[jnp.maximum(own, 0)])
                carry = carry + jnp.where(own >= 0, twice, 0.0)
            return carry
        return lax.fori_loop(0, HALF, one, energy, unroll=2)

    def near_energy(target, source):
        def one(i, energy):
            product = near_product(i)
            target[i] = product
            return energy + fold(product * source[i])
        return lax.fori_loop(0, BLOCKS, one, zero, unroll=4)

    def join(near, i):
        a, b, c = [coupled[e, inverse[e * BLOCKS + i]] for e in range(CROSS)]
        return (near[i] + a) + (b + c)

    zero = jnp.zeros((8, RHS), jnp.float32)

    inputs[0].wait()
    inputs[1].wait()
    for half in range(2):
        def prepare(q, carry):
            gather(0, half, q, lambda j: right_side[j])
            return carry
        lax.fori_loop(0, HALF, prepare, 0)
    pl.semaphore_wait(barrier, n1 + n2 - 2)
    for half in range(2):
        def begin(q, carry):
            send(0, half, q)
            return carry
        lax.fori_loop(0, HALF, begin, 0)
    for copy in inputs[2:]:
        copy.wait()

    lane = lax.broadcasted_iota(jnp.int32, (WIDTH, 2 * WIDTH), 1)

    def both(block):
        twice = jnp.concatenate([block, block], axis=1)
        high = twice.astype(jnp.bfloat16).astype(jnp.float32)
        return jnp.where(lane < WIDTH, high, twice - high).astype(jnp.bfloat16)

    def near_setup(i, carry):
        blocks = [diagonal[i]] + [nearby[i, k] for k in range(LOCAL)]
        for s, block in enumerate(blocks):
            near_lhs[i, :, pl.ds(s * 2 * WIDTH, 2 * WIDTH)] = both(block)
        for s in range(0, SOURCES, 2):
            pair = jnp.concatenate([blocks[s], blocks[min(s + 1, SOURCES - 1)]], axis=1)
            near_lhs[i, :, pl.ds((SOURCES * 2 + s) * WIDTH, 2 * WIDTH)] = pair.astype(jnp.bfloat16)
        return carry

    lax.fori_loop(0, BLOCKS, near_setup, 0, unroll=2)

    def far_setup(t, carry):
        for e in range(CROSS):
            block = remote[0, e, t]
            far_lhs[e, t, :, pl.ds(0, 2 * WIDTH)] = both(block)
            twice = jnp.concatenate([block, block], axis=1)
            far_lhs[e, t, :, pl.ds(2 * WIDTH, 2 * WIDTH)] = twice.astype(jnp.bfloat16)
        return carry

    lax.fori_loop(0, SLOTS, far_setup, 0, unroll=2)

    for e in range(CROSS):
        coupled[e, SLOTS] = jnp.zeros((WIDTH, RHS), jnp.float32)
        owns = [pairs[0, e, 0, t] for t in range(SLOTS)]

        def invert(i, carry):
            found = jnp.int32(SLOTS)
            for t in range(SLOTS):
                found = jnp.where(owns[t] == i, jnp.int32(t), found)
            inverse[e * BLOCKS + i] = found
            return carry
        lax.fori_loop(0, BLOCKS, invert, 0, unroll=4)

    def first_put(i, gamma):
        r = right_side[i]
        put(i, r)
        return gamma + fold(r * r)

    gamma = lax.fori_loop(0, BLOCKS, first_put, zero, unroll=4)

    def near_all(target):
        def one(i, carry):
            target[i] = near_product(i)
            return carry
        lax.fori_loop(0, BLOCKS, one, 0, unroll=4)

    energy = energy_half(0, right_side, near_energy(w0, right_side))
    sum_start(0, 0, rows_of([gamma, energy]))
    far_half(0, 1)

    for half in range(2):
        send_half(1, half, lambda j: join(w0, j))

    def w0_join(i, carry):
        w = join(w0, i)
        w0[i] = w
        put(i, w)
        return carry

    lax.fori_loop(0, BLOCKS, w0_join, 0, unroll=4)
    sum_start(0, 1, sum_finish(0, 0))
    near_all(z0)
    far_half(1, 0)
    totals = sum_finish(0, 1)
    gamma0, delta0 = totals[0:1], totals[1:2]
    step0 = gamma0 / delta0
    far_half(1, 1)

    send_half(2, 0, lambda j: w0[j] - step0 * join(z0, j))

    def z0_join(i, carry):
        zz, wa = join(z0, i), w0[i]
        wb = wa - step0 * zz
        r = right_side[i] - step0 * wa
        z0[i] = zz
        w1[i] = wb
        r1[i] = r
        put(i, wb)
        terms = (r * r, r * wb, r * wa, wb * wb, wb * wa, wa * wa, wb * zz, wa * zz)
        return tuple(c + fold(t) for c, t in zip(carry, terms))

    sums = lax.fori_loop(0, BLOCKS, z0_join, (zero,) * 8, unroll=2)
    sum_start(1, 0, rows_of(sums))

    energy = near_energy(z1, w1)
    sum_start(1, 1, sum_finish(1, 0))
    energy = energy_half(2, w1, energy)
    sum_start(2, 0, rows_of([energy]))
    send_half(2, 1, lambda j: w1[j])
    sum_start(2, 1, sum_finish(2, 0))
    far_half(2, 1)
    totals = sum_finish(1, 1)
    gamma1, delta1, rw0, w1w1, w1w0, w0w0, w1z0, w0z0 = [totals[k : k + 1] for k in range(8)]
    ratio1 = gamma1 / gamma0
    step1 = gamma1 / (delta1 - ratio1 * gamma1 / step0)

    def z1_join(i, carry):
        zz = join(z1, i)
        r, wa, wb, r0 = r1[i], w0[i], w1[i], right_side[i]
        p1 = r + ratio1 * r0
        ap1 = wb + ratio1 * wa
        so_far[i] = step0 * r0 + step1 * p1
        residual[i] = r - step1 * ap1
        image[i] = wb - step1 * (zz + ratio1 * z0[i])
        direction[i] = p1
        dir_image[i] = ap1
        return carry

    lax.fori_loop(0, BLOCKS, z1_join, 0, unroll=4)

    w1aw1 = sum_finish(2, 1)[0:1]
    gamma2 = (
        gamma1
        - 2.0 * step1 * (delta1 + ratio1 * rw0)
        + step1 * step1 * (w1w1 + 2.0 * ratio1 * w1w0 + ratio1 * ratio1 * w0w0)
    )
    delta2 = (
        delta1
        - 2.0 * step1 * (w1w1 + ratio1 * w1w0)
        + step1 * step1 * (w1aw1 + 2.0 * ratio1 * w1z0 + ratio1 * ratio1 * w0z0)
    )
    ratio2 = gamma2 / gamma1
    step2 = gamma2 / (delta2 - ratio2 * gamma2 / step1)

    last_steps[...] = jnp.concatenate([step2, step2 * ratio2, jnp.zeros((6, RHS), jnp.float32)], axis=0)

    for op in range(3):
        def drain(t, carry):
            for e in range(CROSS):
                slot_copy(op, e, t).wait_send()
            return carry
        lax.fori_loop(0, SLOTS, drain, 0)
        for stage in range(2):
            sum_all_wait(op, stage).wait_send()


def solution(mesh):
    nx, nz = mesh.shape["gx"], mesh.shape["gy"] // 8
    n1, n2 = 4 * nx, 2 * nz

    def local(right_side, diagonal_matrices, nearby_coupling_blocks, neighbors, pairs, remote_coupling_blocks):
        field = (BLOCKS, WIDTH, RHS)
        vmem = pl.BlockSpec(memory_space=pltpu.VMEM)
        f32, bf16 = jnp.float32, jnp.bfloat16
        so_far, residual, direction, image, dir_image, last_steps = pl.pallas_call(
            functools.partial(kernel, nx, nz),
            out_shape=(jax.ShapeDtypeStruct(field, f32),) * 5 + (jax.ShapeDtypeStruct((8, RHS), f32),),
            in_specs=[pl.BlockSpec(memory_space=pl.ANY)] * 6,
            out_specs=(vmem,) * 6,
            scratch_shapes=[
                pltpu.SMEM((LOCAL, BLOCKS), jnp.int32),
                pltpu.SMEM(pairs.shape, jnp.int32),
                pltpu.VMEM(field, f32),
                pltpu.VMEM(diagonal_matrices.shape, f32),
                pltpu.VMEM(nearby_coupling_blocks.shape, f32),
                pltpu.VMEM(remote_coupling_blocks.shape, f32),
            ]
            + [pltpu.VMEM(field, f32)] * 5
            + [
                pltpu.VMEM(field, bf16),
                pltpu.VMEM(field, bf16),
                pltpu.VMEM((BLOCKS, WIDTH, 1024), bf16),
                pltpu.VMEM((CROSS, SLOTS, WIDTH, 256), bf16),
                pltpu.VMEM((CROSS, SLOTS + 1, WIDTH, RHS), f32),
                pltpu.VMEM((3, CROSS, SLOTS, WIDTH, RHS), f32),
                pltpu.VMEM((3, CROSS, SLOTS, WIDTH, RHS), f32),
                pltpu.VMEM((3, n1, 8, RHS), f32),
                pltpu.VMEM((3, n2, 8, RHS), f32),
                pltpu.SMEM((CROSS * BLOCKS,), jnp.int32),
                pltpu.SemaphoreType.DMA((6,)),
                pltpu.SemaphoreType.DMA((3, CROSS, SLOTS)),
                pltpu.SemaphoreType.DMA((3, CROSS, SLOTS)),
                pltpu.SemaphoreType.DMA((3,)),
                pltpu.SemaphoreType.DMA((3,)),
                pltpu.SemaphoreType.DMA((3,)),
                pltpu.SemaphoreType.DMA((3,)),
            ],
            compiler_params=pltpu.CompilerParams(
                collective_id=0, has_side_effects=True, vmem_limit_bytes=52 * 1024 * 1024
            ),
            name="relay",
        )(neighbors.T, pairs, right_side, diagonal_matrices, nearby_coupling_blocks, remote_coupling_blocks)
        step, shared = last_steps[0], last_steps[1]
        solution = so_far + (step * residual + shared * direction)
        residual = residual - (step * image + shared * dir_image)
        return solution, residual

    wide = P(("gx", "gy"), None, None)
    return jax.shard_map(
        local,
        mesh=mesh,
        in_specs=(
            wide,
            wide,
            P(("gx", "gy"), None, None, None),
            P(("gx", "gy"), None),
            P(("gx", "gy"), None, None, None),
            P(("gx", "gy"), None, None, None, None),
        ),
        out_specs=(wide, wide),
        check_vma=False,
    )
```

```python
import functools

import jax
import jax.numpy as jnp
from jax import lax
from jax.experimental import pallas as pl
from jax.experimental.pallas import tpu as pltpu
from jax.sharding import PartitionSpec as P

CROSS = 3
SLOTS = 8
HALF = SLOTS // 2
LOCAL = 4
BLOCKS = 16
WIDTH = 64
RHS = 128
SOURCES = LOCAL + 1
DEPTH = 3 * WIDTH
MESH = pl.DeviceIdType.MESH
LEVEL_ORDER = (2, 1, 0)


def tree_sum(parts):
    while len(parts) > 1:
        parts = [parts[i] + parts[i + 1] for i in range(0, len(parts), 2)]
    return parts[0]


def split(value):
    high = value.astype(jnp.bfloat16)
    low = (value - high.astype(jnp.float32)).astype(jnp.bfloat16)
    return high, low


def fold(value):
    return jnp.sum(value.reshape(WIDTH // 8, 8, RHS), axis=0)


def kernel(
    nx, nz,
    neighbors_in, pairs_in, right_side_in, diagonal_in, nearby_in, remote_in,
    w0, w1, z0, z1, factors,
    neighbors, pairs, right_side, diagonal, nearby, remote,
    x_high, x_low, near_lhs, far_lhs, coupled,
    sent, received, first_sums, second_sums, inverse,
    in_sem, send_sem, recv_sem, first_send, first_recv, second_send, second_recv,
):
    gx = lax.axis_index("gx")
    gy = lax.axis_index("gy")
    z, y, core = gy >> 3, (gy >> 1) & 3, gy & 1
    n1, n2 = 4 * nx, 2 * nz
    me1, me2 = gx * 4 + y, z * 2 + core

    def first_peer(k):
        other = jnp.bitwise_xor(me1, k)
        return other >> 2, (z << 3) + ((other & 3) << 1) + core

    def second_peer(k):
        other = jnp.bitwise_xor(me2, k)
        return gx, ((other >> 1) << 3) + (y << 1) + (other & 1)

    barrier = pltpu.get_barrier_semaphore()

    def greet(peer):
        def one(k, carry):
            pl.semaphore_signal(barrier, inc=1, device_id=peer(k), device_id_type=MESH)
            return carry
        return one

    inputs = [
        pltpu.make_async_copy(source, target, in_sem.at[n])
        for n, (source, target) in enumerate(
            (
                (pairs_in, pairs),
                (right_side_in, right_side),
                (neighbors_in, neighbors),
                (diagonal_in, diagonal),
                (nearby_in, nearby),
                (remote_in, remote),
            )
        )
    ]
    for copy in inputs[:2]:
        copy.start()
    lax.fori_loop(1, n1, greet(first_peer), 0)
    lax.fori_loop(1, n2, greet(second_peer), 0)

    bits = [(gy // (1 << e)) % 2 for e in range(CROSS)]

    def slot_copy(op, e, t):
        return pltpu.make_async_remote_copy(
            src_ref=sent.at[op, e, t],
            dst_ref=received.at[op, e, t],
            send_sem=send_sem.at[op, e, t],
            recv_sem=recv_sem.at[op, e, t],
            device_id=(gx, jnp.bitwise_xor(gy, 1 << e)),
            device_id_type=MESH,
        )

    def slot_of(half, q, e):
        return q + (HALF * (1 - bits[e]) if half == 0 else HALF * bits[e])

    def gather(op, half, q, block):
        for e in LEVEL_ORDER:
            t = slot_of(half, q, e)
            sent[op, e, t] = block(jnp.maximum(pairs[0, e, 0, t], 0))

    def send(op, half, q):
        for e in LEVEL_ORDER:
            slot_copy(op, e, slot_of(half, q, e)).start()

    def send_half(op, half, block):
        def one(q, carry):
            gather(op, half, q, block)
            send(op, half, q)
            return carry
        lax.fori_loop(0, HALF, one, 0, unroll=2)

    def sum_copy(index, stage, k):
        buffer, sends, recvs, peer = (
            (first_sums, first_send, first_recv, first_peer),
            (second_sums, second_send, second_recv, second_peer),
        )[stage]
        return pltpu.make_async_remote_copy(
            src_ref=buffer.at[index, 0],
            dst_ref=buffer.at[index, k],
            send_sem=sends.at[index],
            recv_sem=recvs.at[index],
            device_id=peer(k),
            device_id_type=MESH,
        )

    def sum_all_wait(index, stage):
        buffer, sends, recvs, peer = (
            (first_sums, first_send, first_recv, first_peer),
            (second_sums, second_send, second_recv, second_peer),
        )[stage]
        n = (n1, n2)[stage]
        return pltpu.make_async_remote_copy(
            src_ref=buffer.at[index, pl.ds(1, n - 1)],
            dst_ref=buffer.at[index, pl.ds(1, n - 1)],
            send_sem=sends.at[index],
            recv_sem=recvs.at[index],
            device_id=peer(1),
            device_id_type=MESH,
        )

    def sum_start(index, stage, value):
        buffer, n = ((first_sums, n1), (second_sums, n2))[stage]
        buffer[index, 0] = value

        for k in range(n - 1, 0, -1):
            sum_copy(index, stage, k).start()

    def sum_finish(index, stage):
        buffer, n = ((first_sums, n1), (second_sums, n2))[stage]
        sum_all_wait(index, stage).wait_recv()
        return tree_sum([buffer[index, k] for k in range(n)])

    def rows_of(values):
        rows = [jnp.sum(v, axis=0, keepdims=True) for v in values]
        rows += [jnp.zeros((8 - len(rows), RHS), jnp.float32)] if len(rows) < 8 else []
        return jnp.concatenate(rows, axis=0)

    def put(i, value):
        high, low = split(value)
        x_high[i] = high
        x_low[i] = low

    def near_product(i):
        sources = [i] + [jnp.bitwise_and(neighbors[k, i], BLOCKS - 1) for k in range(LOCAL)]
        highs = [x_high[j] for j in sources]
        lows = [x_low[j] for j in sources]
        rhs = jnp.concatenate([h for high in highs for h in (high, high)] + lows, axis=0)
        return jnp.dot(near_lhs[i][:, : SOURCES * DEPTH], rhs, preferred_element_type=jnp.float32)

    def far_product(op, e, t):
        high, low = split(received[op, e, t])
        rhs = jnp.concatenate([high, high, low], axis=0)
        product = jnp.dot(far_lhs[e, t][:, :DEPTH], rhs, preferred_element_type=jnp.float32)
        coupled[e, t] = product
        return product

    def far_step(op, half, q):
        slots = [slot_of(1 - half, q, e) for e in range(CROSS)]
        for e in range(CROSS):
            slot_copy(op, e, slots[e]).wait_recv()
        return slots, [far_product(op, e, slots[e]) for e in range(CROSS)]

    def far_half(op, half):
        def one(q, carry):
            far_step(op, half, q)
            return carry
        lax.fori_loop(0, HALF, one, 0, unroll=2)

    def energy_half(op, source, energy):
        def one(q, carry):
            slots, products = far_step(op, 0, q)
            for e in range(CROSS):
                own = pairs[0, e, 0, slots[e]]
                twice = 2.0 * fold(products[e] * source[jnp.maximum(own, 0)])
                carry = carry + jnp.where(own >= 0, twice, 0.0)
            return carry
        return lax.fori_loop(0, HALF, one, energy, unroll=2)

    def near_energy(target, source):
        def one(i, energy):
            product = near_product(i)
            target[i] = product
            return energy + fold(product * source[i])
        return lax.fori_loop(0, BLOCKS, one, zero, unroll=4)

    def join(near, i):
        a, b, c = [coupled[e, inverse[e * BLOCKS + i]] for e in range(CROSS)]
        return (near[i] + a) + (b + c)

    zero = jnp.zeros((8, RHS), jnp.float32)

    inputs[0].wait()
    inputs[1].wait()
    for copy in inputs[2:]:
        copy.start()
    for half in range(2):
        def prepare(q, carry):
            gather(0, half, q, lambda j: right_side[j])
            return carry
        lax.fori_loop(0, HALF, prepare, 0)
    pl.semaphore_wait(barrier, n1 + n2 - 2)
    for half in range(2):
        def begin(q, carry):
            send(0, half, q)
            return carry
        lax.fori_loop(0, HALF, begin, 0)
    for copy in inputs[2:]:
        copy.wait()

    lane = lax.broadcasted_iota(jnp.int32, (WIDTH, 2 * WIDTH), 1)

    def both(block):
        twice = jnp.concatenate([block, block], axis=1)
        high = twice.astype(jnp.bfloat16).astype(jnp.float32)
        return jnp.where(lane < WIDTH, high, twice - high).astype(jnp.bfloat16)

    def near_setup(i, carry):
        blocks = [diagonal[i]] + [nearby[i, k] for k in range(LOCAL)]
        for s, block in enumerate(blocks):
            near_lhs[i, :, pl.ds(s * 2 * WIDTH, 2 * WIDTH)] = both(block)
        for s in range(0, SOURCES, 2):
            pair = jnp.concatenate([blocks[s], blocks[min(s + 1, SOURCES - 1)]], axis=1)
            near_lhs[i, :, pl.ds((SOURCES * 2 + s) * WIDTH, 2 * WIDTH)] = pair.astype(jnp.bfloat16)
        return carry

    lax.fori_loop(0, BLOCKS, near_setup, 0, unroll=2)

    def far_setup(t, carry):
        for e in range(CROSS):
            block = remote[0, e, t]
            far_lhs[e, t, :, pl.ds(0, 2 * WIDTH)] = both(block)
            twice = jnp.concatenate([block, block], axis=1)
            far_lhs[e, t, :, pl.ds(2 * WIDTH, 2 * WIDTH)] = twice.astype(jnp.bfloat16)
        return carry

    lax.fori_loop(0, SLOTS, far_setup, 0, unroll=2)

    for e in range(CROSS):
        coupled[e, SLOTS] = jnp.zeros((WIDTH, RHS), jnp.float32)
        owns = [pairs[0, e, 0, t] for t in range(SLOTS)]

        def invert(i, carry):
            found = jnp.int32(SLOTS)
            for t in range(SLOTS):
                found = jnp.where(owns[t] == i, jnp.int32(t), found)
            inverse[e * BLOCKS + i] = found
            return carry
        lax.fori_loop(0, BLOCKS, invert, 0, unroll=4)

    def first_put(i, gamma):
        r = right_side[i]
        put(i, r)
        return gamma + fold(r * r)

    gamma = lax.fori_loop(0, BLOCKS, first_put, zero, unroll=4)

    def near_all(target):
        def one(i, carry):
            target[i] = near_product(i)
            return carry
        lax.fori_loop(0, BLOCKS, one, 0, unroll=4)

    energy = energy_half(0, right_side, near_energy(w0, right_side))
    sum_start(0, 0, rows_of([gamma, energy]))
    far_half(0, 1)

    for half in range(2):
        send_half(1, half, lambda j: join(w0, j))

    def w0_join(i, carry):
        w = join(w0, i)
        w0[i] = w
        put(i, w)
        return carry

    lax.fori_loop(0, BLOCKS, w0_join, 0, unroll=4)
    sum_start(0, 1, sum_finish(0, 0))
    near_all(z0)
    far_half(1, 0)
    totals = sum_finish(0, 1)
    gamma0, delta0 = totals[0:1], totals[1:2]
    step0 = gamma0 / delta0
    far_half(1, 1)

    send_half(2, 0, lambda j: w0[j] - step0 * join(z0, j))

    def z0_join(i, carry):
        zz, wa = join(z0, i), w0[i]
        wb = wa - step0 * zz
        r = right_side[i] - step0 * wa
        z0[i] = zz
        w1[i] = wb
        put(i, wb)
        terms = (r * r, r * wb, wb * wb, wb * wa, wa * wa, wb * zz, wa * zz)
        return tuple(c + fold(t) for c, t in zip(carry, terms))

    sums = lax.fori_loop(0, BLOCKS, z0_join, (zero,) * 7, unroll=2)
    energy = energy_half(2, w1, near_energy(z1, w1))
    sum_start(1, 0, rows_of(list(sums) + [energy]))
    send_half(2, 1, lambda j: w1[j])
    sum_start(1, 1, sum_finish(1, 0))
    far_half(2, 1)

    def z1_join(i, carry):
        z1[i] = join(z1, i)
        return carry

    lax.fori_loop(0, BLOCKS, z1_join, 0, unroll=4)
    totals = sum_finish(1, 1)
    gamma1, delta1, w1w1, w1w0, w0w0, w1z0, w0z0, w1aw1 = [totals[k : k + 1] for k in range(8)]
    rw0 = delta0 - step0 * w0w0
    ratio1 = gamma1 / gamma0
    step1 = gamma1 / (delta1 - ratio1 * gamma1 / step0)
    gamma2 = (
        gamma1
        - 2.0 * step1 * (delta1 + ratio1 * rw0)
        + step1 * step1 * (w1w1 + 2.0 * ratio1 * w1w0 + ratio1 * ratio1 * w0w0)
    )
    delta2 = (
        delta1
        - 2.0 * step1 * (w1w1 + ratio1 * w1w0)
        + step1 * step1 * (w1aw1 + 2.0 * ratio1 * w1z0 + ratio1 * ratio1 * w0z0)
    )
    ratio2 = gamma2 / gamma1
    step2 = gamma2 / (delta2 - ratio2 * gamma2 / step1)
    both_steps = step1 * step2
    factors[...] = jnp.concatenate(
        [
            step0 + step1 * (1.0 + ratio1) + step2 * (1.0 + ratio2 * (1.0 + ratio1)),
            step0 * (step1 + step2 * (1.0 + ratio2)) + both_steps * ratio1,
            both_steps,
            step0 + ratio1 * (step1 + step2 * ratio2),
            step1 + step2 * (1.0 + ratio2),
            both_steps * ratio1,
            jnp.zeros((2, RHS), jnp.float32),
        ],
        axis=0,
    )

    for op in range(3):
        def drain(t, carry):
            for e in range(CROSS):
                slot_copy(op, e, t).wait_send()
            return carry
        lax.fori_loop(0, SLOTS, drain, 0)
    for index in range(2):
        for stage in range(2):
            sum_all_wait(index, stage).wait_send()


def solution(mesh):
    nx, nz = mesh.shape["gx"], mesh.shape["gy"] // 8
    n1, n2 = 4 * nx, 2 * nz

    def local(right_side, diagonal_matrices, nearby_coupling_blocks, neighbors, pairs, remote_coupling_blocks):
        field = (BLOCKS, WIDTH, RHS)
        vmem = pl.BlockSpec(memory_space=pltpu.VMEM)
        f32, bf16 = jnp.float32, jnp.bfloat16
        w0, w1, z0, z1, factors = pl.pallas_call(
            functools.partial(kernel, nx, nz),
            out_shape=(jax.ShapeDtypeStruct(field, f32),) * 4 + (jax.ShapeDtypeStruct((8, RHS), f32),),
            in_specs=[pl.BlockSpec(memory_space=pl.ANY)] * 6,
            out_specs=(vmem,) * 5,
            scratch_shapes=[
                pltpu.SMEM((LOCAL, BLOCKS), jnp.int32),
                pltpu.SMEM(pairs.shape, jnp.int32),
                pltpu.VMEM(field, f32),
                pltpu.VMEM(diagonal_matrices.shape, f32),
                pltpu.VMEM(nearby_coupling_blocks.shape, f32),
                pltpu.VMEM(remote_coupling_blocks.shape, f32),
            ]
            + [
                pltpu.VMEM(field, bf16),
                pltpu.VMEM(field, bf16),
                pltpu.VMEM((BLOCKS, WIDTH, 1024), bf16),
                pltpu.VMEM((CROSS, SLOTS, WIDTH, 256), bf16),
                pltpu.VMEM((CROSS, SLOTS + 1, WIDTH, RHS), f32),
                pltpu.VMEM((3, CROSS, SLOTS, WIDTH, RHS), f32),
                pltpu.VMEM((3, CROSS, SLOTS, WIDTH, RHS), f32),
                pltpu.VMEM((2, n1, 8, RHS), f32),
                pltpu.VMEM((2, n2, 8, RHS), f32),
                pltpu.SMEM((CROSS * BLOCKS,), jnp.int32),
                pltpu.SemaphoreType.DMA((6,)),
                pltpu.SemaphoreType.DMA((3, CROSS, SLOTS)),
                pltpu.SemaphoreType.DMA((3, CROSS, SLOTS)),
                pltpu.SemaphoreType.DMA((2,)),
                pltpu.SemaphoreType.DMA((2,)),
                pltpu.SemaphoreType.DMA((2,)),
                pltpu.SemaphoreType.DMA((2,)),
            ],
            compiler_params=pltpu.CompilerParams(
                collective_id=0, has_side_effects=True, vmem_limit_bytes=51 * 1024 * 1024
            ),
            name="relay",
        )(neighbors.T, pairs, right_side, diagonal_matrices, nearby_coupling_blocks, remote_coupling_blocks)
        solution = (factors[0] * right_side - factors[1] * w0) - factors[2] * w1
        residual = ((right_side - factors[3] * w0) - factors[4] * w1) + (factors[5] * z0 + factors[2] * z1)
        return solution, residual

    wide = P(("gx", "gy"), None, None)
    return jax.shard_map(
        local,
        mesh=mesh,
        in_specs=(
            wide,
            wide,
            P(("gx", "gy"), None, None, None),
            P(("gx", "gy"), None),
            P(("gx", "gy"), None, None, None),
            P(("gx", "gy"), None, None, None, None),
        ),
        out_specs=(wide, wide),
        check_vma=False,
    )
```

```python
import functools

import jax
import jax.numpy as jnp
from jax import lax
from jax.experimental import pallas as pl
from jax.experimental.pallas import tpu as pltpu
from jax.sharding import PartitionSpec as P

CROSS = 3
SLOTS = 8
HALF = SLOTS // 2
LOCAL = 4
BLOCKS = 16
WIDTH = 64
RHS = 128
SOURCES = LOCAL + 1
DEPTH = 4 * WIDTH
MESH = pl.DeviceIdType.MESH
LEVEL_ORDER = (2, 1, 0)


def tree_sum(parts):
    while len(parts) > 1:
        parts = [parts[i] + parts[i + 1] for i in range(0, len(parts), 2)]
    return parts[0]


def split(value):
    parts = []
    for _ in range(3):
        parts.append(value.astype(jnp.bfloat16))
        value = value - parts[-1].astype(jnp.float32)
    return parts


def product(tiles, parts):
    lhs, rhs = [], []
    for tile, (high, mid, low) in zip(tiles, parts):
        lhs += [tile[:, : 2 * WIDTH], tile]
        rhs += [high, high, mid, mid, low, high]
    return jnp.dot(
        jnp.concatenate(lhs, axis=1), jnp.concatenate(rhs, axis=0), preferred_element_type=jnp.float32
    )


def fold(value):
    return jnp.sum(value.reshape(WIDTH // 8, 8, RHS), axis=0)


def kernel(
    nx, nz,
    neighbors_in, pairs_in, right_side_in, diagonal_in, nearby_in, remote_in,
    w0, w1, z0, z1, factors,
    neighbors, pairs, right_side, diagonal, nearby, remote,
    x_high, x_mid, x_low, near_lhs, far_lhs, coupled,
    sent, received, first_sums, second_sums, inverse,
    in_sem, send_sem, recv_sem, first_send, first_recv, second_send, second_recv,
):
    gx = lax.axis_index("gx")
    gy = lax.axis_index("gy")
    z, y, core = gy >> 3, (gy >> 1) & 3, gy & 1
    n1, n2 = 4 * nx, 2 * nz
    me1, me2 = gx * 4 + y, z * 2 + core

    def first_peer(k):
        other = jnp.bitwise_xor(me1, k)
        return other >> 2, (z << 3) + ((other & 3) << 1) + core

    def second_peer(k):
        other = jnp.bitwise_xor(me2, k)
        return gx, ((other >> 1) << 3) + (y << 1) + (other & 1)

    barrier = pltpu.get_barrier_semaphore()

    def greet(peer):
        def one(k, carry):
            pl.semaphore_signal(barrier, inc=1, device_id=peer(k), device_id_type=MESH)
            return carry
        return one

    inputs = [
        pltpu.make_async_copy(source, target, in_sem.at[n])
        for n, (source, target) in enumerate(
            (
                (pairs_in, pairs),
                (right_side_in, right_side),
                (neighbors_in, neighbors),
                (diagonal_in, diagonal),
                (nearby_in, nearby),
                (remote_in, remote),
            )
        )
    ]
    for copy in inputs[:2]:
        copy.start()
    lax.fori_loop(1, n1, greet(first_peer), 0)
    lax.fori_loop(1, n2, greet(second_peer), 0)

    bits = [(gy // (1 << e)) % 2 for e in range(CROSS)]

    def slot_copy(op, e, t):
        return pltpu.make_async_remote_copy(
            src_ref=sent.at[op, e, t],
            dst_ref=received.at[op, e, t],
            send_sem=send_sem.at[op, e, t],
            recv_sem=recv_sem.at[op, e, t],
            device_id=(gx, jnp.bitwise_xor(gy, 1 << e)),
            device_id_type=MESH,
        )

    def slot_of(half, q, e):
        return q + (HALF * (1 - bits[e]) if half == 0 else HALF * bits[e])

    def gather(op, half, q, block):
        for e in LEVEL_ORDER:
            t = slot_of(half, q, e)
            sent[op, e, t] = block(jnp.maximum(pairs[0, e, 0, t], 0))

    def send(op, half, q):
        for e in LEVEL_ORDER:
            slot_copy(op, e, slot_of(half, q, e)).start()

    def send_half(op, half, block):
        def one(q, carry):
            gather(op, half, q, block)
            send(op, half, q)
            return carry
        lax.fori_loop(0, HALF, one, 0, unroll=4)

    def sum_copy(index, stage, k):
        buffer, sends, recvs, peer = (
            (first_sums, first_send, first_recv, first_peer),
            (second_sums, second_send, second_recv, second_peer),
        )[stage]
        return pltpu.make_async_remote_copy(
            src_ref=buffer.at[index, 0],
            dst_ref=buffer.at[index, k],
            send_sem=sends.at[index],
            recv_sem=recvs.at[index],
            device_id=peer(k),
            device_id_type=MESH,
        )

    def sum_all_wait(index, stage):
        buffer, sends, recvs, peer = (
            (first_sums, first_send, first_recv, first_peer),
            (second_sums, second_send, second_recv, second_peer),
        )[stage]
        n = (n1, n2)[stage]
        return pltpu.make_async_remote_copy(
            src_ref=buffer.at[index, pl.ds(1, n - 1)],
            dst_ref=buffer.at[index, pl.ds(1, n - 1)],
            send_sem=sends.at[index],
            recv_sem=recvs.at[index],
            device_id=peer(1),
            device_id_type=MESH,
        )

    def sum_start(index, stage, value):
        buffer, n = ((first_sums, n1), (second_sums, n2))[stage]
        buffer[index, 0] = value

        for k in range(n - 1, 0, -1):
            sum_copy(index, stage, k).start()

    def sum_finish(index, stage):
        buffer, n = ((first_sums, n1), (second_sums, n2))[stage]
        sum_all_wait(index, stage).wait_recv()
        return tree_sum([buffer[index, k] for k in range(n)])

    def rows_of(values):
        rows = [jnp.sum(v, axis=0, keepdims=True) for v in values]
        rows += [jnp.zeros((8 - len(rows), RHS), jnp.float32)] if len(rows) < 8 else []
        return jnp.concatenate(rows, axis=0)

    def put(i, value):
        for store, part in zip((x_high, x_mid, x_low), split(value)):
            store[i] = part

    def near_product(i):
        sources = [i] + [jnp.bitwise_and(neighbors[k, i], BLOCKS - 1) for k in range(LOCAL)]
        parts = [(x_high[j], x_mid[j], x_low[j]) for j in sources]
        return product([near_lhs[i, s] for s in range(SOURCES)], parts)

    def far_product(op, e, t):
        result = product([far_lhs[e, t]], [split(received[op, e, t])])
        coupled[e, t] = result
        return result

    def far_step(op, half, q):
        slots = [slot_of(1 - half, q, e) for e in range(CROSS)]
        for e in range(CROSS):
            slot_copy(op, e, slots[e]).wait_recv()
        return slots, [far_product(op, e, slots[e]) for e in range(CROSS)]

    def far_half(op, half):
        def one(q, carry):
            far_step(op, half, q)
            return carry
        lax.fori_loop(0, HALF, one, 0, unroll=4)

    def energy_half(op, source, energy):
        def one(q, carry):
            slots, products = far_step(op, 0, q)
            for e in range(CROSS):
                own = pairs[0, e, 0, slots[e]]
                twice = 2.0 * fold(products[e] * source[jnp.maximum(own, 0)])
                carry = carry + jnp.where(own >= 0, twice, 0.0)
            return carry
        return lax.fori_loop(0, HALF, one, energy, unroll=4)

    def near_energy(target, source):
        def one(i, energy):
            result = near_product(i)
            target[i] = result
            return energy + fold(result * source[i])
        return lax.fori_loop(0, BLOCKS, one, zero, unroll=4)

    def join(near, i):
        a, b, c = [coupled[e, inverse[e * BLOCKS + i]] for e in range(CROSS)]
        return (near[i] + a) + (b + c)

    zero = jnp.zeros((8, RHS), jnp.float32)

    inputs[0].wait()
    inputs[1].wait()
    for copy in inputs[2:]:
        copy.start()
    for half in range(2):
        def prepare(q, carry):
            gather(0, half, q, lambda j: right_side[j])
            return carry
        lax.fori_loop(0, HALF, prepare, 0)
    pl.semaphore_wait(barrier, n1 + n2 - 2)
    for half in range(2):
        def begin(q, carry):
            send(0, half, q)
            return carry
        lax.fori_loop(0, HALF, begin, 0)
    for copy in inputs[2:]:
        copy.wait()

    lane = lax.broadcasted_iota(jnp.int32, (WIDTH, 2 * WIDTH), 1)

    def tile(block):
        twice = jnp.concatenate([block, block], axis=1)
        high, mid, low = [part.astype(jnp.float32) for part in split(twice)]
        pieces = [jnp.where(lane < WIDTH, high, other) for other in (mid, low)]
        return jnp.concatenate(pieces, axis=1).astype(jnp.bfloat16)

    def near_setup(i, carry):
        near_lhs[i, 0] = tile(diagonal[i])
        for k in range(LOCAL):
            near_lhs[i, k + 1] = tile(nearby[i, k])
        return carry

    lax.fori_loop(0, BLOCKS, near_setup, 0, unroll=2)

    def far_setup(t, carry):
        for e in range(CROSS):
            far_lhs[e, t] = tile(remote[0, e, t])
        return carry

    lax.fori_loop(0, SLOTS, far_setup, 0, unroll=2)

    for e in range(CROSS):
        coupled[e, SLOTS] = jnp.zeros((WIDTH, RHS), jnp.float32)
        owns = [pairs[0, e, 0, t] for t in range(SLOTS)]

        def invert(i, carry):
            found = jnp.int32(SLOTS)
            for t in range(SLOTS):
                found = jnp.where(owns[t] == i, jnp.int32(t), found)
            inverse[e * BLOCKS + i] = found
            return carry
        lax.fori_loop(0, BLOCKS, invert, 0, unroll=4)

    def first_put(i, gamma):
        r = right_side[i]
        put(i, r)
        return gamma + fold(r * r)

    gamma = lax.fori_loop(0, BLOCKS, first_put, zero, unroll=4)

    def near_all(target):
        def one(i, carry):
            target[i] = near_product(i)
            return carry
        lax.fori_loop(0, BLOCKS, one, 0, unroll=4)

    energy = energy_half(0, right_side, near_energy(w0, right_side))
    sum_start(0, 0, rows_of([gamma, energy]))
    far_half(0, 1)

    for half in range(2):
        send_half(1, half, lambda j: join(w0, j))

    def w0_join(i, carry):
        w = join(w0, i)
        w0[i] = w
        put(i, w)
        return carry

    lax.fori_loop(0, BLOCKS, w0_join, 0, unroll=4)
    sum_start(0, 1, sum_finish(0, 0))
    near_all(z0)
    far_half(1, 0)
    totals = sum_finish(0, 1)
    gamma0, delta0 = totals[0:1], totals[1:2]
    step0 = gamma0 / delta0
    far_half(1, 1)

    send_half(2, 0, lambda j: w0[j] - step0 * join(z0, j))

    def z0_join(i, carry):
        zz, wa = join(z0, i), w0[i]
        wb = wa - step0 * zz
        r = right_side[i] - step0 * wa
        z0[i] = zz
        w1[i] = wb
        put(i, wb)
        terms = (r * r, r * wb, wb * wb, wb * wa, wa * wa, wb * zz, wa * zz)
        return tuple(c + fold(t) for c, t in zip(carry, terms))

    sums = lax.fori_loop(0, BLOCKS, z0_join, (zero,) * 7, unroll=2)
    energy = energy_half(2, w1, near_energy(z1, w1))
    sum_start(1, 0, rows_of(list(sums) + [energy]))
    send_half(2, 1, lambda j: w1[j])
    sum_start(1, 1, sum_finish(1, 0))
    far_half(2, 1)

    def z1_join(i, carry):
        z1[i] = join(z1, i)
        return carry

    lax.fori_loop(0, BLOCKS, z1_join, 0, unroll=4)
    totals = sum_finish(1, 1)
    gamma1, delta1, w1w1, w1w0, w0w0, w1z0, w0z0, w1aw1 = [totals[k : k + 1] for k in range(8)]
    rw0 = delta0 - step0 * w0w0
    ratio1 = gamma1 / gamma0
    step1 = gamma1 / (delta1 - ratio1 * gamma1 / step0)
    gamma2 = (
        gamma1
        - 2.0 * step1 * (delta1 + ratio1 * rw0)
        + step1 * step1 * (w1w1 + 2.0 * ratio1 * w1w0 + ratio1 * ratio1 * w0w0)
    )
    delta2 = (
        delta1
        - 2.0 * step1 * (w1w1 + ratio1 * w1w0)
        + step1 * step1 * (w1aw1 + 2.0 * ratio1 * w1z0 + ratio1 * ratio1 * w0z0)
    )
    ratio2 = gamma2 / gamma1
    step2 = gamma2 / (delta2 - ratio2 * gamma2 / step1)
    both_steps = step1 * step2
    factors[...] = jnp.concatenate(
        [
            step0 + step1 * (1.0 + ratio1) + step2 * (1.0 + ratio2 * (1.0 + ratio1)),
            step0 * (step1 + step2 * (1.0 + ratio2)) + both_steps * ratio1,
            both_steps,
            step0 + ratio1 * (step1 + step2 * ratio2),
            step1 + step2 * (1.0 + ratio2),
            both_steps * ratio1,
            jnp.zeros((2, RHS), jnp.float32),
        ],
        axis=0,
    )

    for op in range(3):
        def drain(t, carry):
            for e in range(CROSS):
                slot_copy(op, e, t).wait_send()
            return carry
        lax.fori_loop(0, SLOTS, drain, 0)
    for index in range(2):
        for stage in range(2):
            sum_all_wait(index, stage).wait_send()


def solution(mesh):
    nx, nz = mesh.shape["gx"], mesh.shape["gy"] // 8
    n1, n2 = 4 * nx, 2 * nz

    def local(right_side, diagonal_matrices, nearby_coupling_blocks, neighbors, pairs, remote_coupling_blocks):
        field = (BLOCKS, WIDTH, RHS)
        vmem = pl.BlockSpec(memory_space=pltpu.VMEM)
        f32, bf16 = jnp.float32, jnp.bfloat16
        w0, w1, z0, z1, factors = pl.pallas_call(
            functools.partial(kernel, nx, nz),
            out_shape=(jax.ShapeDtypeStruct(field, f32),) * 4 + (jax.ShapeDtypeStruct((8, RHS), f32),),
            in_specs=[pl.BlockSpec(memory_space=pl.ANY)] * 6,
            out_specs=(vmem,) * 5,
            scratch_shapes=[
                pltpu.SMEM((LOCAL, BLOCKS), jnp.int32),
                pltpu.SMEM(pairs.shape, jnp.int32),
                pltpu.VMEM(field, f32),
                pltpu.VMEM(diagonal_matrices.shape, f32),
                pltpu.VMEM(nearby_coupling_blocks.shape, f32),
                pltpu.VMEM(remote_coupling_blocks.shape, f32),
            ]
            + [
                pltpu.VMEM(field, bf16),
                pltpu.VMEM(field, bf16),
                pltpu.VMEM(field, bf16),
                pltpu.VMEM((BLOCKS, SOURCES, WIDTH, DEPTH), bf16),
                pltpu.VMEM((CROSS, SLOTS, WIDTH, DEPTH), bf16),
                pltpu.VMEM((CROSS, SLOTS + 1, WIDTH, RHS), f32),
                pltpu.VMEM((3, CROSS, SLOTS, WIDTH, RHS), f32),
                pltpu.VMEM((3, CROSS, SLOTS, WIDTH, RHS), f32),
                pltpu.VMEM((2, n1, 8, RHS), f32),
                pltpu.VMEM((2, n2, 8, RHS), f32),
                pltpu.SMEM((CROSS * BLOCKS,), jnp.int32),
                pltpu.SemaphoreType.DMA((6,)),
                pltpu.SemaphoreType.DMA((3, CROSS, SLOTS)),
                pltpu.SemaphoreType.DMA((3, CROSS, SLOTS)),
                pltpu.SemaphoreType.DMA((2,)),
                pltpu.SemaphoreType.DMA((2,)),
                pltpu.SemaphoreType.DMA((2,)),
                pltpu.SemaphoreType.DMA((2,)),
            ],
            compiler_params=pltpu.CompilerParams(
                collective_id=0, has_side_effects=True, vmem_limit_bytes=54_000_000
            ),
            name="relay",
        )(neighbors.T, pairs, right_side, diagonal_matrices, nearby_coupling_blocks, remote_coupling_blocks)
        solution = (factors[0] * right_side - factors[1] * w0) - factors[2] * w1
        residual = ((right_side - factors[3] * w0) - factors[4] * w1) + (factors[5] * z0 + factors[2] * z1)
        return solution, residual

    wide = P(("gx", "gy"), None, None)
    return jax.shard_map(
        local,
        mesh=mesh,
        in_specs=(
            wide,
            wide,
            P(("gx", "gy"), None, None, None),
            P(("gx", "gy"), None),
            P(("gx", "gy"), None, None, None),
            P(("gx", "gy"), None, None, None, None),
        ),
        out_specs=(wide, wide),
        check_vma=False,
    )
```

```python
import functools

import jax
import jax.numpy as jnp
from jax import lax
from jax.experimental import pallas as pl
from jax.experimental.pallas import tpu as pltpu
from jax.sharding import PartitionSpec as P

CROSS = 3
SLOTS = 8
HALF = SLOTS // 2
LOCAL = 4
BLOCKS = 16
WIDTH = 64
RHS = 128
SOURCES = LOCAL + 1
DEPTH = 4 * WIDTH
MESH = pl.DeviceIdType.MESH
LEVEL_ORDER = (2, 1, 0)


def tree_sum(parts):
    while len(parts) > 1:
        parts = [parts[i] + parts[i + 1] for i in range(0, len(parts), 2)]
    return parts[0]


def split(value):
    parts = []
    for _ in range(3):
        parts.append(value.astype(jnp.bfloat16))
        value = value - parts[-1].astype(jnp.float32)
    return parts


def product(tiles, parts):
    lhs, rhs = [], []
    for tile, (high, mid, low) in zip(tiles, parts):
        lhs += [tile[:, : 2 * WIDTH], tile]
        rhs += [high, high, mid, mid, low, high]
    return jnp.dot(
        jnp.concatenate(lhs, axis=1), jnp.concatenate(rhs, axis=0), preferred_element_type=jnp.float32
    )


def fold(value):
    return jnp.sum(value.reshape(WIDTH // 8, 8, RHS), axis=0)


def kernel(
    nx, nz,
    table_in, right_side_in, diagonal_in, nearby_in, remote_in,
    w0, w1, z0, z1, factors,
    table, right_side, diagonal, nearby, remote,
    x_high, x_mid, x_low, near_lhs, far_lhs, coupled,
    sent, received, first_sums, second_sums, inverse,
    in_sem, send_sem, recv_sem, first_send, first_recv, second_send, second_recv,
):
    gx = lax.axis_index("gx")
    gy = lax.axis_index("gy")
    z, y, core = gy >> 3, (gy >> 1) & 3, gy & 1
    n1, n2 = 4 * nx, 2 * nz
    me1, me2 = gx * 4 + y, z * 2 + core

    def first_peer(k):
        other = jnp.bitwise_xor(me1, k)
        return other >> 2, (z << 3) + ((other & 3) << 1) + core

    def second_peer(k):
        other = jnp.bitwise_xor(me2, k)
        return gx, ((other >> 1) << 3) + (y << 1) + (other & 1)

    barrier = pltpu.get_barrier_semaphore()

    def greet(peer):
        def one(k, carry):
            pl.semaphore_signal(barrier, inc=1, device_id=peer(k), device_id_type=MESH)
            return carry
        return one

    inputs = [
        pltpu.make_async_copy(source, target, in_sem.at[n])
        for n, (source, target) in enumerate(
            (
                (table_in, table),
                (right_side_in, right_side),
                (diagonal_in, diagonal),
                (nearby_in, nearby),
                (remote_in, remote),
            )
        )
    ]
    for copy in inputs[:2]:
        copy.start()
    lax.fori_loop(1, n1, greet(first_peer), 0)
    lax.fori_loop(1, n2, greet(second_peer), 0)

    bits = [(gy // (1 << e)) % 2 for e in range(CROSS)]

    def slot_copy(op, e, t):
        return pltpu.make_async_remote_copy(
            src_ref=sent.at[op, e, t],
            dst_ref=received.at[op, e, t],
            send_sem=send_sem.at[op, e, t],
            recv_sem=recv_sem.at[op, e, t],
            device_id=(gx, jnp.bitwise_xor(gy, 1 << e)),
            device_id_type=MESH,
        )

    def slot_of(half, q, e):
        return q + (HALF * (1 - bits[e]) if half == 0 else HALF * bits[e])

    def gather(op, half, q, block):
        for e in LEVEL_ORDER:
            t = slot_of(half, q, e)
            sent[op, e, t] = block(jnp.maximum(table[e, 0, t], 0))

    def send(op, half, q):
        for e in LEVEL_ORDER:
            slot_copy(op, e, slot_of(half, q, e)).start()

    def send_half(op, half, block):
        def one(q, carry):
            gather(op, half, q, block)
            send(op, half, q)
            return carry
        lax.fori_loop(0, HALF, one, 0, unroll=4)

    def sum_copy(index, stage, k):
        buffer, sends, recvs, peer = (
            (first_sums, first_send, first_recv, first_peer),
            (second_sums, second_send, second_recv, second_peer),
        )[stage]
        return pltpu.make_async_remote_copy(
            src_ref=buffer.at[index, 0],
            dst_ref=buffer.at[index, k],
            send_sem=sends.at[index],
            recv_sem=recvs.at[index],
            device_id=peer(k),
            device_id_type=MESH,
        )

    def sum_all_wait(index, stage):
        buffer, sends, recvs, peer = (
            (first_sums, first_send, first_recv, first_peer),
            (second_sums, second_send, second_recv, second_peer),
        )[stage]
        n = (n1, n2)[stage]
        return pltpu.make_async_remote_copy(
            src_ref=buffer.at[index, pl.ds(1, n - 1)],
            dst_ref=buffer.at[index, pl.ds(1, n - 1)],
            send_sem=sends.at[index],
            recv_sem=recvs.at[index],
            device_id=peer(1),
            device_id_type=MESH,
        )

    def sum_start(index, stage, value):
        buffer, n = ((first_sums, n1), (second_sums, n2))[stage]
        buffer[index, 0] = value

        for k in range(n - 1, 0, -1):
            sum_copy(index, stage, k).start()

    def sum_finish(index, stage):
        buffer, n = ((first_sums, n1), (second_sums, n2))[stage]
        sum_all_wait(index, stage).wait_recv()
        return tree_sum([buffer[index, k] for k in range(n)])

    def rows_of(values):
        rows = [jnp.sum(v, axis=0, keepdims=True) for v in values]
        rows += [jnp.zeros((8 - len(rows), RHS), jnp.float32)] if len(rows) < 8 else []
        return jnp.concatenate(rows, axis=0)

    def put(i, value):
        for store, part in zip((x_high, x_mid, x_low), split(value)):
            store[i] = part

    def near_product(i):
        sources = [i] + [jnp.bitwise_and(table[CROSS + k // 2, k % 2, i], BLOCKS - 1) for k in range(LOCAL)]
        parts = [(x_high[j], x_mid[j], x_low[j]) for j in sources]
        return product([near_lhs[i, s] for s in range(SOURCES)], parts)

    def far_product(op, e, t):
        result = product([far_lhs[e, t]], [split(received[op, e, t])])
        coupled[e, t] = result
        return result

    def far_step(op, half, q):
        slots = [slot_of(1 - half, q, e) for e in range(CROSS)]
        for e in range(CROSS):
            slot_copy(op, e, slots[e]).wait_recv()
        return slots, [far_product(op, e, slots[e]) for e in range(CROSS)]

    def far_half(op, half):
        def one(q, carry):
            far_step(op, half, q)
            return carry
        lax.fori_loop(0, HALF, one, 0, unroll=4)

    def energy_half(op, source, energy):
        def one(q, carry):
            slots, products = far_step(op, 0, q)
            for e in range(CROSS):
                own = table[e, 0, slots[e]]
                twice = 2.0 * fold(products[e] * source[jnp.maximum(own, 0)])
                carry = carry + jnp.where(own >= 0, twice, 0.0)
            return carry
        return lax.fori_loop(0, HALF, one, energy, unroll=4)

    def near_energy(target, source):
        def one(i, energy):
            result = near_product(i)
            target[i] = result
            return energy + fold(result * source[i])
        return lax.fori_loop(0, BLOCKS, one, zero, unroll=4)

    def join(near, i):
        a, b, c = [coupled[e, inverse[e * BLOCKS + i]] for e in range(CROSS)]
        return (near[i] + a) + (b + c)

    zero = jnp.zeros((8, RHS), jnp.float32)

    inputs[0].wait()
    inputs[1].wait()
    for copy in inputs[2:]:
        copy.start()
    for half in range(2):
        def prepare(q, carry):
            gather(0, half, q, lambda j: right_side[j])
            return carry
        lax.fori_loop(0, HALF, prepare, 0)
    pl.semaphore_wait(barrier, n1 + n2 - 2)
    for half in range(2):
        def begin(q, carry):
            send(0, half, q)
            return carry
        lax.fori_loop(0, HALF, begin, 0)
    for copy in inputs[2:]:
        copy.wait()

    lane = lax.broadcasted_iota(jnp.int32, (WIDTH, 2 * WIDTH), 1)

    def tile(block):
        twice = jnp.concatenate([block, block], axis=1)
        high, mid, low = [part.astype(jnp.float32) for part in split(twice)]
        pieces = [jnp.where(lane < WIDTH, high, other) for other in (mid, low)]
        return jnp.concatenate(pieces, axis=1).astype(jnp.bfloat16)

    def near_setup(i, carry):
        near_lhs[i, 0] = tile(diagonal[i])
        for k in range(LOCAL):
            near_lhs[i, k + 1] = tile(nearby[i, k])
        return carry

    lax.fori_loop(0, BLOCKS, near_setup, 0, unroll=2)

    def far_setup(t, carry):
        for e in range(CROSS):
            far_lhs[e, t] = tile(remote[0, e, t])
        return carry

    lax.fori_loop(0, SLOTS, far_setup, 0, unroll=2)

    for e in range(CROSS):
        coupled[e, SLOTS] = jnp.zeros((WIDTH, RHS), jnp.float32)
        owns = [table[e, 0, t] for t in range(SLOTS)]

        def invert(i, carry):
            found = jnp.int32(SLOTS)
            for t in range(SLOTS):
                found = jnp.where(owns[t] == i, jnp.int32(t), found)
            inverse[e * BLOCKS + i] = found
            return carry
        lax.fori_loop(0, BLOCKS, invert, 0, unroll=4)

    def first_put(i, gamma):
        r = right_side[i]
        put(i, r)
        return gamma + fold(r * r)

    gamma = lax.fori_loop(0, BLOCKS, first_put, zero, unroll=4)

    def near_all(target):
        def one(i, carry):
            target[i] = near_product(i)
            return carry
        lax.fori_loop(0, BLOCKS, one, 0, unroll=4)

    energy = energy_half(0, right_side, near_energy(w0, right_side))
    sum_start(0, 0, rows_of([gamma, energy]))
    far_half(0, 1)

    for half in range(2):
        send_half(1, half, lambda j: join(w0, j))

    def w0_join(i, carry):
        w = join(w0, i)
        w0[i] = w
        put(i, w)
        return carry

    lax.fori_loop(0, BLOCKS, w0_join, 0, unroll=4)
    sum_start(0, 1, sum_finish(0, 0))
    near_all(z0)
    far_half(1, 0)
    totals = sum_finish(0, 1)
    gamma0, delta0 = totals[0:1], totals[1:2]
    step0 = gamma0 / delta0
    far_half(1, 1)

    send_half(2, 0, lambda j: w0[j] - step0 * join(z0, j))

    def z0_join(i, carry):
        zz, wa = join(z0, i), w0[i]
        wb = wa - step0 * zz
        r = right_side[i] - step0 * wa
        z0[i] = zz
        w1[i] = wb
        put(i, wb)
        terms = (r * r, r * wb, wb * wb, wb * wa, wa * wa, wb * zz, wa * zz)
        return tuple(c + fold(t) for c, t in zip(carry, terms))

    sums = lax.fori_loop(0, BLOCKS, z0_join, (zero,) * 7, unroll=2)
    energy = energy_half(2, w1, near_energy(z1, w1))
    sum_start(1, 0, rows_of(list(sums) + [energy]))
    send_half(2, 1, lambda j: w1[j])
    sum_start(1, 1, sum_finish(1, 0))
    far_half(2, 1)

    def z1_join(i, carry):
        z1[i] = join(z1, i)
        return carry

    lax.fori_loop(0, BLOCKS, z1_join, 0, unroll=4)
    totals = sum_finish(1, 1)
    gamma1, delta1, w1w1, w1w0, w0w0, w1z0, w0z0, w1aw1 = [totals[k : k + 1] for k in range(8)]
    rw0 = delta0 - step0 * w0w0
    ratio1 = gamma1 / gamma0
    step1 = gamma1 / (delta1 - ratio1 * gamma1 / step0)
    gamma2 = (
        gamma1
        - 2.0 * step1 * (delta1 + ratio1 * rw0)
        + step1 * step1 * (w1w1 + 2.0 * ratio1 * w1w0 + ratio1 * ratio1 * w0w0)
    )
    delta2 = (
        delta1
        - 2.0 * step1 * (w1w1 + ratio1 * w1w0)
        + step1 * step1 * (w1aw1 + 2.0 * ratio1 * w1z0 + ratio1 * ratio1 * w0z0)
    )
    ratio2 = gamma2 / gamma1
    step2 = gamma2 / (delta2 - ratio2 * gamma2 / step1)
    both_steps = step1 * step2
    factors[...] = jnp.concatenate(
        [
            step0 + step1 * (1.0 + ratio1) + step2 * (1.0 + ratio2 * (1.0 + ratio1)),
            step0 * (step1 + step2 * (1.0 + ratio2)) + both_steps * ratio1,
            both_steps,
            step0 + ratio1 * (step1 + step2 * ratio2),
            step1 + step2 * (1.0 + ratio2),
            both_steps * ratio1,
            jnp.zeros((2, RHS), jnp.float32),
        ],
        axis=0,
    )

    for op in range(3):
        def drain(t, carry):
            for e in range(CROSS):
                slot_copy(op, e, t).wait_send()
            return carry
        lax.fori_loop(0, SLOTS, drain, 0)
    for index in range(2):
        for stage in range(2):
            sum_all_wait(index, stage).wait_send()


def solution(mesh):
    nx, nz = mesh.shape["gx"], mesh.shape["gy"] // 8
    n1, n2 = 4 * nx, 2 * nz

    def local(right_side, diagonal_matrices, nearby_coupling_blocks, neighbors, pairs, remote_coupling_blocks):
        field = (BLOCKS, WIDTH, RHS)
        vmem = pl.BlockSpec(memory_space=pltpu.VMEM)
        f32, bf16 = jnp.float32, jnp.bfloat16
        own_pairs = jnp.pad(pairs[0], ((0, 0), (0, 0), (0, BLOCKS - SLOTS)))
        table = jnp.concatenate([own_pairs, neighbors.T.reshape(LOCAL // 2, 2, BLOCKS)])
        w0, w1, z0, z1, factors = pl.pallas_call(
            functools.partial(kernel, nx, nz),
            out_shape=(jax.ShapeDtypeStruct(field, f32),) * 4 + (jax.ShapeDtypeStruct((8, RHS), f32),),
            in_specs=[pl.BlockSpec(memory_space=pl.ANY)] * 5,
            out_specs=(vmem,) * 5,
            scratch_shapes=[
                pltpu.SMEM(table.shape, jnp.int32),
                pltpu.VMEM(field, f32),
                pltpu.VMEM(diagonal_matrices.shape, f32),
                pltpu.VMEM(nearby_coupling_blocks.shape, f32),
                pltpu.VMEM(remote_coupling_blocks.shape, f32),
            ]
            + [
                pltpu.VMEM(field, bf16),
                pltpu.VMEM(field, bf16),
                pltpu.VMEM(field, bf16),
                pltpu.VMEM((BLOCKS, SOURCES, WIDTH, DEPTH), bf16),
                pltpu.VMEM((CROSS, SLOTS, WIDTH, DEPTH), bf16),
                pltpu.VMEM((CROSS, SLOTS + 1, WIDTH, RHS), f32),
                pltpu.VMEM((3, CROSS, SLOTS, WIDTH, RHS), f32),
                pltpu.VMEM((3, CROSS, SLOTS, WIDTH, RHS), f32),
                pltpu.VMEM((2, n1, 8, RHS), f32),
                pltpu.VMEM((2, n2, 8, RHS), f32),
                pltpu.SMEM((CROSS * BLOCKS,), jnp.int32),
                pltpu.SemaphoreType.DMA((5,)),
                pltpu.SemaphoreType.DMA((3, CROSS, SLOTS)),
                pltpu.SemaphoreType.DMA((3, CROSS, SLOTS)),
                pltpu.SemaphoreType.DMA((2,)),
                pltpu.SemaphoreType.DMA((2,)),
                pltpu.SemaphoreType.DMA((2,)),
                pltpu.SemaphoreType.DMA((2,)),
            ],
            compiler_params=pltpu.CompilerParams(
                collective_id=0, has_side_effects=True, vmem_limit_bytes=54_000_000
            ),
            name="relay",
        )(table, right_side, diagonal_matrices, nearby_coupling_blocks, remote_coupling_blocks)
        solution = (factors[0] * right_side - factors[1] * w0) - factors[2] * w1
        residual = ((right_side - factors[3] * w0) - factors[4] * w1) + (factors[5] * z0 + factors[2] * z1)
        return solution, residual

    wide = P(("gx", "gy"), None, None)
    return jax.shard_map(
        local,
        mesh=mesh,
        in_specs=(
            wide,
            wide,
            P(("gx", "gy"), None, None, None),
            P(("gx", "gy"), None),
            P(("gx", "gy"), None, None, None),
            P(("gx", "gy"), None, None, None, None),
        ),
        out_specs=(wide, wide),
        check_vma=False,
    )
```

```python
import functools

import jax
import jax.numpy as jnp
from jax import lax
from jax.experimental import pallas as pl
from jax.experimental.pallas import tpu as pltpu
from jax.sharding import PartitionSpec as P

CROSS = 3
SLOTS = 8
HALF = SLOTS // 2
LOCAL = 4
BLOCKS = 16
WIDTH = 64
RHS = 128
SOURCES = LOCAL + 1
DEPTH = 4 * WIDTH
MESH = pl.DeviceIdType.MESH
LEVEL_ORDER = (2, 1, 0)


def tree_sum(parts):
    while len(parts) > 1:
        parts = [parts[i] + parts[i + 1] for i in range(0, len(parts), 2)]
    return parts[0]


def split(value):
    parts = []
    for _ in range(3):
        parts.append(value.astype(jnp.bfloat16))
        value = value - parts[-1].astype(jnp.float32)
    return parts


def product(tiles, parts):
    lhs, rhs = [], []
    for tile, (high, mid, low) in zip(tiles, parts):
        lhs += [tile[:, : 2 * WIDTH], tile]
        rhs += [high, high, mid, mid, low, high]
    return jnp.dot(
        jnp.concatenate(lhs, axis=1), jnp.concatenate(rhs, axis=0), preferred_element_type=jnp.float32
    )


def fold(value):
    return jnp.sum(value.reshape(WIDTH // 8, 8, RHS), axis=0)


def kernel(
    nx, nz,
    table_in, right_side_in, diagonal_in, nearby_in, remote_in,
    w0, w1, z0, z1, factors,
    table, right_side, diagonal, nearby, remote,
    x_high, x_mid, x_low, near_lhs, far_lhs, coupled,
    sent, received, first_sums, second_sums, inverse,
    in_sem, send_sem, recv_sem, first_send, first_recv, second_send, second_recv,
):
    gx = lax.axis_index("gx")
    gy = lax.axis_index("gy")
    z, y, core = gy >> 3, (gy >> 1) & 3, gy & 1
    n1, n2 = 4 * nx, 2 * nz
    me1, me2 = gx * 4 + y, z * 2 + core

    def first_peer(k):
        other = jnp.bitwise_xor(me1, k)
        return other >> 2, (z << 3) + ((other & 3) << 1) + core

    def second_peer(k):
        other = jnp.bitwise_xor(me2, k)
        return gx, ((other >> 1) << 3) + (y << 1) + (other & 1)

    barrier = pltpu.get_barrier_semaphore()

    def greet(peer):
        def one(k, carry):
            pl.semaphore_signal(barrier, inc=1, device_id=peer(k), device_id_type=MESH)
            return carry
        return one

    inputs = [
        pltpu.make_async_copy(source, target, in_sem.at[n])
        for n, (source, target) in enumerate(
            (
                (table_in, table),
                (right_side_in, right_side),
                (diagonal_in, diagonal),
                (nearby_in, nearby),
                (remote_in, remote),
            )
        )
    ]
    for copy in inputs[:2]:
        copy.start()
    lax.fori_loop(1, n1, greet(first_peer), 0)
    lax.fori_loop(1, n2, greet(second_peer), 0)

    bits = [(gy // (1 << e)) % 2 for e in range(CROSS)]

    def slot_copy(op, e, t):
        return pltpu.make_async_remote_copy(
            src_ref=sent.at[op, e, t],
            dst_ref=received.at[op, e, t],
            send_sem=send_sem.at[op, e, t],
            recv_sem=recv_sem.at[op, e, t],
            device_id=(gx, jnp.bitwise_xor(gy, 1 << e)),
            device_id_type=MESH,
        )

    def slot_of(half, q, e):
        return q + (HALF * (1 - bits[e]) if half == 0 else HALF * bits[e])

    def gather(op, half, q, block):
        for e in LEVEL_ORDER:
            t = slot_of(half, q, e)
            sent[op, e, t] = block(jnp.maximum(table[e, 0, t], 0))

    def send(op, half, q):
        for e in LEVEL_ORDER:
            slot_copy(op, e, slot_of(half, q, e)).start()

    def send_half(op, half, block):
        def one(q, carry):
            gather(op, half, q, block)
            send(op, half, q)
            return carry
        lax.fori_loop(0, HALF, one, 0, unroll=4)

    def sum_copy(index, stage, k):
        buffer, sends, recvs, peer = (
            (first_sums, first_send, first_recv, first_peer),
            (second_sums, second_send, second_recv, second_peer),
        )[stage]
        return pltpu.make_async_remote_copy(
            src_ref=buffer.at[index, 0],
            dst_ref=buffer.at[index, k],
            send_sem=sends.at[index],
            recv_sem=recvs.at[index],
            device_id=peer(k),
            device_id_type=MESH,
        )

    def sum_all_wait(index, stage):
        buffer, sends, recvs, peer = (
            (first_sums, first_send, first_recv, first_peer),
            (second_sums, second_send, second_recv, second_peer),
        )[stage]
        n = (n1, n2)[stage]
        return pltpu.make_async_remote_copy(
            src_ref=buffer.at[index, pl.ds(1, n - 1)],
            dst_ref=buffer.at[index, pl.ds(1, n - 1)],
            send_sem=sends.at[index],
            recv_sem=recvs.at[index],
            device_id=peer(1),
            device_id_type=MESH,
        )

    def sum_start(index, stage, value):
        buffer, n = ((first_sums, n1), (second_sums, n2))[stage]
        buffer[index, 0] = value

        for k in range(n - 1, 0, -1):
            sum_copy(index, stage, k).start()

    def sum_finish(index, stage):
        buffer, n = ((first_sums, n1), (second_sums, n2))[stage]
        sum_all_wait(index, stage).wait_recv()
        return tree_sum([buffer[index, k] for k in range(n)])

    def rows_of(values):
        rows = [jnp.sum(v, axis=0, keepdims=True) for v in values]
        rows += [jnp.zeros((8 - len(rows), RHS), jnp.float32)] if len(rows) < 8 else []
        return jnp.concatenate(rows, axis=0)

    def put(i, value):
        for store, part in zip((x_high, x_mid, x_low), split(value)):
            store[i] = part

    def near_product(i):
        sources = [i] + [jnp.bitwise_and(table[CROSS + k // 2, k % 2, i], BLOCKS - 1) for k in range(LOCAL)]
        parts = [(x_high[j], x_mid[j], x_low[j]) for j in sources]
        return product([near_lhs[i, s] for s in range(SOURCES)], parts)

    def far_product(op, e, t):
        result = product([far_lhs[e, t]], [split(received[op, e, t])])
        coupled[e, t] = result
        return result

    def far_step(op, half, q):
        slots = [slot_of(1 - half, q, e) for e in range(CROSS)]
        for e in range(CROSS):
            slot_copy(op, e, slots[e]).wait_recv()
        return slots, [far_product(op, e, slots[e]) for e in range(CROSS)]

    def far_half(op, half):
        def one(q, carry):
            far_step(op, half, q)
            return carry
        lax.fori_loop(0, HALF, one, 0, unroll=4)

    def energy_half(op, source, weigh, energy):
        def one(q, carry):
            slots, products = far_step(op, 0, q)
            for e in range(CROSS):
                own = table[e, 0, slots[e]]
                twice = 2.0 * fold(weigh(products[e], source[jnp.maximum(own, 0)]))
                carry = carry + jnp.where(own >= 0, twice, 0.0)
            return carry
        return lax.fori_loop(0, HALF, one, energy, unroll=4)

    def near_energy(target, source, weigh):
        def one(i, energy):
            result = near_product(i)
            target[i] = result
            return energy + fold(weigh(result, source[i]))
        return lax.fori_loop(0, BLOCKS, one, zero, unroll=4)

    def join(near, i):
        a, b, c = [coupled[e, inverse[e * BLOCKS + i]] for e in range(CROSS)]
        return (near[i] + a) + (b + c)

    zero = jnp.zeros((8, RHS), jnp.float32)

    inputs[0].wait()
    inputs[1].wait()
    for copy in inputs[2:]:
        copy.start()
    for half in range(2):
        def prepare(q, carry):
            gather(0, half, q, lambda j: right_side[j])
            return carry
        lax.fori_loop(0, HALF, prepare, 0)
    pl.semaphore_wait(barrier, n1 + n2 - 2)
    for half in range(2):
        def begin(q, carry):
            send(0, half, q)
            return carry
        lax.fori_loop(0, HALF, begin, 0)
    for copy in inputs[2:]:
        copy.wait()

    lane = lax.broadcasted_iota(jnp.int32, (WIDTH, 2 * WIDTH), 1)

    def tile(block):
        twice = jnp.concatenate([block, block], axis=1)
        high, mid, low = [part.astype(jnp.float32) for part in split(twice)]
        pieces = [jnp.where(lane < WIDTH, high, other) for other in (mid, low)]
        return jnp.concatenate(pieces, axis=1).astype(jnp.bfloat16)

    def near_setup(i, carry):
        near_lhs[i, 0] = tile(diagonal[i])
        for k in range(LOCAL):
            near_lhs[i, k + 1] = tile(nearby[i, k])
        return carry

    lax.fori_loop(0, BLOCKS, near_setup, 0, unroll=2)

    def far_setup(t, carry):
        for e in range(CROSS):
            far_lhs[e, t] = tile(remote[0, e, t])
        return carry

    lax.fori_loop(0, SLOTS, far_setup, 0, unroll=2)

    for e in range(CROSS):
        coupled[e, SLOTS] = jnp.zeros((WIDTH, RHS), jnp.float32)
        owns = [table[e, 0, t] for t in range(SLOTS)]

        def invert(i, carry):
            found = jnp.int32(SLOTS)
            for t in range(SLOTS):
                found = jnp.where(owns[t] == i, jnp.int32(t), found)
            inverse[e * BLOCKS + i] = found
            return carry
        lax.fori_loop(0, BLOCKS, invert, 0, unroll=4)

    def first_put(i, gamma):
        r = right_side[i]
        put(i, r)
        return gamma + fold(r * r)

    gamma = lax.fori_loop(0, BLOCKS, first_put, zero, unroll=4)

    def near_all(target):
        def one(i, carry):
            target[i] = near_product(i)
            return carry
        lax.fori_loop(0, BLOCKS, one, 0, unroll=4)

    energy = energy_half(0, right_side, jnp.multiply, near_energy(w0, right_side, jnp.multiply))
    sum_start(0, 0, rows_of([gamma, energy]))
    far_half(0, 1)

    for half in range(2):
        send_half(1, half, lambda j: join(w0, j))

    def w0_join(i, carry):
        w = join(w0, i)
        w0[i] = w
        put(i, w)
        return carry

    lax.fori_loop(0, BLOCKS, w0_join, 0, unroll=4)
    sum_start(0, 1, sum_finish(0, 0))
    near_all(z0)
    far_half(1, 0)
    totals = sum_finish(0, 1)
    gamma0, delta0 = totals[0:1], totals[1:2]
    step0 = gamma0 / delta0
    far_half(1, 1)

    send_half(2, 0, lambda j: w0[j] - step0 * join(z0, j))

    def scaled(image, value):
        return (step0 * (step0 * image)) * (step0 * value)

    def z0_join(i, carry):
        zz, wa = join(z0, i), w0[i]
        wb = wa - step0 * zz
        r = right_side[i] - step0 * wa
        z0[i] = zz
        w1[i] = wb
        put(i, wb)
        wa, wb, zz = step0 * wa, step0 * wb, step0 * (step0 * zz)
        terms = (r * r, r * wb, wb * wb, wb * wa, wa * wa, wb * zz, wa * zz)
        return tuple(c + fold(t) for c, t in zip(carry, terms))

    sums = lax.fori_loop(0, BLOCKS, z0_join, (zero,) * 7, unroll=2)
    energy = energy_half(2, w1, scaled, near_energy(z1, w1, scaled))
    sum_start(1, 0, rows_of(list(sums) + [energy]))
    send_half(2, 1, lambda j: w1[j])
    sum_start(1, 1, sum_finish(1, 0))
    far_half(2, 1)

    def z1_join(i, carry):
        z1[i] = join(z1, i)
        return carry

    lax.fori_loop(0, BLOCKS, z1_join, 0, unroll=4)
    totals = sum_finish(1, 1)
    gamma1, delta1, w1w1, w1w0, w0w0, w1z0, w0z0, w1aw1 = [totals[k : k + 1] for k in range(8)]
    rw0 = gamma0 - w0w0
    ratio1 = gamma1 / gamma0
    pace1 = gamma1 / (delta1 - ratio1 * gamma1)
    gamma2 = (
        gamma1
        - 2.0 * pace1 * (delta1 + ratio1 * rw0)
        + pace1 * pace1 * (w1w1 + 2.0 * ratio1 * w1w0 + ratio1 * ratio1 * w0w0)
    )
    delta2 = (
        delta1
        - 2.0 * pace1 * (w1w1 + ratio1 * w1w0)
        + pace1 * pace1 * (w1aw1 + 2.0 * ratio1 * w1z0 + ratio1 * ratio1 * w0z0)
    )
    ratio2 = gamma2 / gamma1
    pace2 = gamma2 / (delta2 - ratio2 * gamma2 / pace1)
    step1, step2 = step0 * pace1, step0 * pace2
    both_steps = step1 * step2
    factors[...] = jnp.concatenate(
        [
            step0 + step1 * (1.0 + ratio1) + step2 * (1.0 + ratio2 * (1.0 + ratio1)),
            step0 * (step1 + step2 * (1.0 + ratio2)) + both_steps * ratio1,
            both_steps,
            step0 + ratio1 * (step1 + step2 * ratio2),
            step1 + step2 * (1.0 + ratio2),
            both_steps * ratio1,
            jnp.zeros((2, RHS), jnp.float32),
        ],
        axis=0,
    )

    for op in range(3):
        def drain(t, carry):
            for e in range(CROSS):
                slot_copy(op, e, t).wait_send()
            return carry
        lax.fori_loop(0, SLOTS, drain, 0)
    for index in range(2):
        for stage in range(2):
            sum_all_wait(index, stage).wait_send()


def solution(mesh):
    nx, nz = mesh.shape["gx"], mesh.shape["gy"] // 8
    n1, n2 = 4 * nx, 2 * nz

    def local(right_side, diagonal_matrices, nearby_coupling_blocks, neighbors, pairs, remote_coupling_blocks):
        field = (BLOCKS, WIDTH, RHS)
        vmem = pl.BlockSpec(memory_space=pltpu.VMEM)
        f32, bf16 = jnp.float32, jnp.bfloat16
        own_pairs = jnp.pad(pairs[0], ((0, 0), (0, 0), (0, BLOCKS - SLOTS)))
        table = jnp.concatenate([own_pairs, neighbors.T.reshape(LOCAL // 2, 2, BLOCKS)])
        w0, w1, z0, z1, factors = pl.pallas_call(
            functools.partial(kernel, nx, nz),
            out_shape=(jax.ShapeDtypeStruct(field, f32),) * 4 + (jax.ShapeDtypeStruct((8, RHS), f32),),
            in_specs=[pl.BlockSpec(memory_space=pl.ANY)] * 5,
            out_specs=(vmem,) * 5,
            scratch_shapes=[
                pltpu.SMEM(table.shape, jnp.int32),
                pltpu.VMEM(field, f32),
                pltpu.VMEM(diagonal_matrices.shape, f32),
                pltpu.VMEM(nearby_coupling_blocks.shape, f32),
                pltpu.VMEM(remote_coupling_blocks.shape, f32),
            ]
            + [
                pltpu.VMEM(field, bf16),
                pltpu.VMEM(field, bf16),
                pltpu.VMEM(field, bf16),
                pltpu.VMEM((BLOCKS, SOURCES, WIDTH, DEPTH), bf16),
                pltpu.VMEM((CROSS, SLOTS, WIDTH, DEPTH), bf16),
                pltpu.VMEM((CROSS, SLOTS + 1, WIDTH, RHS), f32),
                pltpu.VMEM((3, CROSS, SLOTS, WIDTH, RHS), f32),
                pltpu.VMEM((3, CROSS, SLOTS, WIDTH, RHS), f32),
                pltpu.VMEM((2, n1, 8, RHS), f32),
                pltpu.VMEM((2, n2, 8, RHS), f32),
                pltpu.SMEM((CROSS * BLOCKS,), jnp.int32),
                pltpu.SemaphoreType.DMA((5,)),
                pltpu.SemaphoreType.DMA((3, CROSS, SLOTS)),
                pltpu.SemaphoreType.DMA((3, CROSS, SLOTS)),
                pltpu.SemaphoreType.DMA((2,)),
                pltpu.SemaphoreType.DMA((2,)),
                pltpu.SemaphoreType.DMA((2,)),
                pltpu.SemaphoreType.DMA((2,)),
            ],
            compiler_params=pltpu.CompilerParams(
                collective_id=0, has_side_effects=True, vmem_limit_bytes=54_000_000
            ),
            name="relay",
        )(table, right_side, diagonal_matrices, nearby_coupling_blocks, remote_coupling_blocks)
        solution = (factors[0] * right_side - factors[1] * w0) - factors[2] * w1
        residual = ((right_side - factors[3] * w0) - factors[4] * w1) + (factors[5] * z0 + factors[2] * z1)
        return solution, residual

    wide = P(("gx", "gy"), None, None)
    return jax.shard_map(
        local,
        mesh=mesh,
        in_specs=(
            wide,
            wide,
            P(("gx", "gy"), None, None, None),
            P(("gx", "gy"), None),
            P(("gx", "gy"), None, None, None),
            P(("gx", "gy"), None, None, None, None),
        ),
        out_specs=(wide, wide),
        check_vma=False,
    )
```
